32 devices in a mesh: ctx: 8 (over y, x, core), head: 4 (over z).
Axes of the slice: x: 2, y: 2, z: 4, core: 2. Of those that a mesh axis runs over, the one named last changes fastest.
Arguments:
- queries: bfloat16 [16384, 4096], P('ctx', 'head'), may hold values from -2 to 2
- key_rows: bfloat16 [16384, 4096], P('ctx', 'head'), may hold values from -2 to 2
- value_rows: bfloat16 [16384, 4096], P('ctx', 'head'), may hold values from -6 to 6
- log_decay: bfloat16 [16384, 32], P('ctx', 'head'), may hold values from -0.4 to 0, as said below
- norm_gain: float32 [4096], P('head'), may hold values from 0.1 to 1.9
- doc_lengths: int32 [16], replicated, may hold values from 1 to 8192, 16384 in all
- packing: int32 [128], replicated, may hold values from 0 to 127, as said below
Outputs:
- mixed: bfloat16 [16384, 4096], P('ctx', 'head')
The draws below stay inside these ranges and needn't reach their ends.
Inputs may be any that keep to these rules, and one draw needn't show every extreme that they name: packing is a permutation of the blocks. Loader block b is block b % 16 of ctx device b // 16; packed block p belongs to owner p // 16. Of the blocks of one loader, each owner receives none or exactly 4. `doc_lengths`: the lengths sum to 16384; the longest is 8192. `log_decay`: negative logarithms of decays.
All inputs are finite; a program needn't handle non-finite values.
Results may differ from the reference program's by a relative error of at most 0.0055.
Values may be sent and summed in bfloat16 or wider, within the bound.
A program may use at most 192 MiB of HBM per device.

```python
import math
import jax
import jax.numpy as jnp
import numpy as np
from jax import lax

HEADS = 32
HD = 128
BLOCK = 128
SEGMENT_TOKENS = 2048
BLK_DEV = 16
WINDOW_TOKENS = 16384
NBLK = 128
CAP = 4
DOCS = 16
N_CTX = 8


def draw_packing(key, part):
    devices = WINDOW_TOKENS // SEGMENT_TOKENS
    blocks = SEGMENT_TOKENS // BLOCK
    groups = blocks // CAP
    first_key, second_key, third_key = jax.random.split(jax.random.fold_in(key, 11), 3)
    scores = jax.random.permutation(first_key, devices).astype(jnp.int32)
    offset_ids = jnp.arange(devices, dtype=jnp.int32)
    scores = jnp.where(offset_ids == 1, -2, scores)
    scores = jnp.where(offset_ids == devices // 2, -1, scores)
    chosen = jnp.argsort(scores, stable=True)[:groups].astype(jnp.int32)
    document_offsets = jax.random.permutation(third_key, chosen)
    loader = jnp.arange(devices, dtype=jnp.int32)[:, None]
    local = jnp.arange(blocks, dtype=jnp.int32)[None, :]
    owner = (loader + document_offsets[local // CAP]) % devices
    owner_keys = jax.random.split(second_key, devices)
    orders = jax.vmap(lambda single: jax.random.permutation(single, blocks))(owner_keys)
    position = orders[owner, jnp.broadcast_to(local, owner.shape)]
    return (owner * blocks + position).reshape(-1).astype(jnp.int32)


def draw_log_decay(key, part):
    segment_count = jax.random.split(jax.random.fold_in(key, 23), 6)
    share = 0.5
    fast = jax.random.uniform(segment_count[0], (HEADS,)) < share
    fast_rate = jnp.exp(jax.random.uniform(segment_count[1], (HEADS,), minval=math.log(1.0 / 50.0), maxval=math.log(1.0 / 30.0)))
    slow_rate = jnp.exp(jax.random.uniform(segment_count[2], (HEADS,), minval=math.log(0.2 / WINDOW_TOKENS), maxval=math.log(1.2 / WINDOW_TOKENS)))
    base = jnp.where(fast, fast_rate, slow_rate)
    per_block = jnp.exp(jax.random.uniform(segment_count[3], (WINDOW_TOKENS // BLOCK, 1, HEADS), minval=math.log(0.6), maxval=math.log(1.5)))
    per_row = jnp.exp(jax.random.uniform(segment_count[4], (WINDOW_TOKENS // BLOCK, BLOCK, HEADS), minval=math.log(0.7), maxval=math.log(1.4)))
    decay_rate = (base[None, None, :] * per_block * per_row).reshape(WINDOW_TOKENS, HEADS)
    token_span = jax.random.uniform(segment_count[5], (WINDOW_TOKENS, 1)) < 3.0 / WINDOW_TOKENS
    return (-(decay_rate + jnp.where(token_span, 0.29, 0.0))).astype(jnp.bfloat16)


def steps_of(rng, extent, cuts, low, top_value):
    def one(axis_at, shards_of):
        heights = jax.random.uniform(jax.random.fold_in(jax.random.fold_in(rng, 6), axis_at), (shards_of,), jnp.float32, low / len(cuts), top_value / len(cuts))
        return jnp.repeat(jnp.exp(heights), extent[axis_at] // shards_of).reshape((-1,) + (1,) * (len(extent) - axis_at - 1))

    factor_of = one(*cuts[0])
    for cut in cuts[1:]:
        factor_of = factor_of * one(*cut)
    return factor_of


def profile(amount, total, reach, lean):
    portions = [(1 << 20) // math.isqrt(grade ** lean) + 1 for grade in range(2, amount + 1)]
    rest, counts = total - reach - (amount - 1), [1] * (amount - 1)
    while rest > 0:
        movable = [i for i in range(amount - 1) if counts[i] < reach]
        pool, remaining = sum([portions[i] for i in movable]), rest
        for i in movable:
            addition = min(reach - counts[i], max(1, remaining * portions[i] // pool), rest)
            counts[i] = counts[i] + addition
            rest = rest - addition
    return np.array([reach] + counts)


def ragged_sizes(key, count, total, bound, lean):
    if count == 2:
        one = jax.random.randint(key, (), max(1, total - bound), min(bound, total - 1) + 1)
        return jnp.stack([one, total - one])
    sizes = jnp.asarray(profile(count, total, bound, lean), jnp.int32)
    pairs = (count - 1) // 2
    source_of, taker = sizes[1:1 + 2 * pairs:2], sizes[2:2 + 2 * pairs:2]
    room = jnp.minimum(source_of - 1, bound - taker)
    moved = jax.random.randint(jax.random.fold_in(key, 1), (pairs,), 0, 1 << 20) % (room + 1)
    sizes = sizes.at[1:1 + 2 * pairs:2].set(source_of - moved).at[2:2 + 2 * pairs:2].set(taker + moved)
    return sizes[jax.random.permutation(jax.random.fold_in(key, 2), count)]


def normal_values(rng, extent, deviation, most, cuts=(), held_as=jnp.bfloat16):
    values = jax.random.normal(rng, extent, jnp.float32) * deviation
    if len(cuts) > 0:
        values = steps_of(rng, extent, cuts, -0.22, 0.18) * values
    return jnp.clip(values, min=-most, max=most).astype(held_as)


def setup_inputs(seed: int = 0) -> dict:
    seeds = jax.random.split(jax.random.key(seed), 8)
    queries = normal_values(seeds[0], (WINDOW_TOKENS, HEADS * HD), 0.3, 2.0, ((0, 8), (1, 4)))
    key_rows = normal_values(seeds[1], (WINDOW_TOKENS, HEADS * HD), 0.3, 2.0, ((0, 8), (1, 4)))
    value_rows = normal_values(seeds[2], (WINDOW_TOKENS, HEADS * HD), 1.0, 6.0, ((0, 8), (1, 4)))
    log_decay = draw_log_decay(jax.random.fold_in(seeds[7], 71), 0)
    norm_gain = jnp.clip(1.0 + 0.18 * jax.random.normal(seeds[4], (HEADS * HD,), jnp.float32), 0.1, 1.9)
    doc_lengths = ragged_sizes(seeds[5], DOCS, WINDOW_TOKENS, WINDOW_TOKENS // 2, 2).astype(jnp.int32)
    packing = draw_packing(jax.random.fold_in(seeds[7], 71), 0)
    return {"queries": queries, "key_rows": key_rows, "value_rows": value_rows, "log_decay": log_decay, "norm_gain": norm_gain, "doc_lengths": doc_lengths, "packing": packing}


def rounded(values):
    return lax.optimization_barrier(values.astype(jnp.bfloat16)).astype(jnp.float32)

def local_pass(query_blocks, key_blocks, value_blocks, decay_blocks, first, docid):
    length = first.shape[1]
    block_log = jnp.cumsum(decay_blocks.astype(jnp.float32), axis=1)
    block_total = block_log[:, -1, :]
    seen = jnp.cumsum(first, axis=1)
    reach_block = (seen == 0).astype(jnp.float32)
    unbroken = (seen[:, -1] == 0).astype(jnp.float32)
    order = jnp.arange(length)
    causal = order[:, None] >= order[None, :]
    allowed = causal[None] & (docid[:, :, None] == docid[:, None, :])
    by_head = jnp.transpose(block_log, (0, 2, 1))
    gaps = by_head[:, :, :, None] - by_head[:, :, None, :]
    weight = jnp.where(allowed[:, None], jnp.exp(jnp.minimum(gaps, 0.0)), 0.0)
    queries32 = query_blocks.astype(jnp.float32)
    keys_float32 = key_blocks.astype(jnp.float32)
    values32 = value_blocks.astype(jnp.float32)
    scores = jnp.einsum('nthd,nshd->nhts', queries32, keys_float32)
    weights = rounded(scores * weight)
    intra = jnp.einsum('nhts,nshd->nthd', weights, values32)
    same_last = (docid == docid[:, -1:]).astype(jnp.float32)
    keep = jnp.exp(block_total[:, None, :] - block_log) * same_last[:, :, None]
    key_decayed = rounded(keys_float32 * keep[..., None])
    own = jnp.einsum('nshd,nshe->nhde', key_decayed, values32)
    gate = jnp.exp(block_total) * unbroken[:, None]

    def advance(state, item):
        factor, term = item
        return (factor[:, None, None] * state + term, state)
    start = jnp.zeros(own.shape[1:], jnp.float32)
    s_end, states = lax.scan(advance, start, (gate, own))
    query_decayed = rounded(queries32 * (jnp.exp(block_log) * reach_block[:, :, None])[..., None])
    inter = jnp.einsum('nthd,nhde->nthe', query_decayed, rounded(states))
    prior = jnp.cumsum(block_total, axis=0) - block_total
    segment_log = block_log + prior[:, None, :]
    block_starts = seen[:, -1]
    before = jnp.cumsum(block_starts) - block_starts
    reach_segment = (seen + before[:, None] == 0).astype(jnp.float32)
    clean = (jnp.sum(first) == 0).astype(jnp.float32)
    decay_all = jnp.exp(segment_log[-1, -1]) * clean
    return (intra + inter, segment_log, reach_segment, decay_all, s_end)

def reference(queries, key_rows, value_rows, log_decay, norm_gain, doc_lengths, packing):
    width = HEADS * HD
    inverse = jnp.argsort(packing).astype(jnp.int32)

    def pack(values, inner):
        moved = values.reshape(NBLK, BLOCK, values.shape[1])[inverse]
        return moved.reshape((N_CTX, BLK_DEV, BLOCK) + inner)
    query_seg = pack(queries, (HEADS, HD))
    key_seg = pack(key_rows, (HEADS, HD))
    value_seg = pack(value_rows, (HEADS, HD))
    decay_seg = pack(log_decay, (HEADS,))
    starts = jnp.cumsum(doc_lengths) - doc_lengths
    positions = jnp.arange(WINDOW_TOKENS)
    first = jnp.any(positions[:, None] == starts[None, :], axis=1).astype(jnp.int32)
    docid = lax.optimization_barrier(jnp.sum((starts[None, :] <= positions[:, None]).astype(jnp.int32), axis=1)) - 1
    first = first.reshape(N_CTX, BLK_DEV, BLOCK)
    docid = docid.reshape(N_CTX, BLK_DEV, BLOCK)

    def summary(items):
        outcome = local_pass(*items)
        return (outcome[3], outcome[4])
    decays, ends = lax.map(summary, (query_seg, key_seg, value_seg, decay_seg, first, docid))

    def handoff(state, item):
        factor, term = item
        return (factor[:, None, None] * state + term, state)
    zero_state = jnp.zeros((HEADS, HD, HD), jnp.float32)
    last_state, incoming = lax.scan(handoff, zero_state, (decays, ends))

    def finish(items):
        query_blocks = items[0]
        arrival = items[6]
        local_out, segment_log, reach_segment, decay_all, s_end = local_pass(*items[:6])
        scaled = rounded(query_blocks.astype(jnp.float32) * (jnp.exp(segment_log) * reach_segment[:, :, None])[..., None])
        carried = jnp.einsum('nthd,hde->nthe', scaled, rounded(arrival))
        total = (local_out + carried).reshape(SEGMENT_TOKENS, width)
        square_mean = lax.optimization_barrier(jnp.mean(total * total, axis=1, keepdims=True))
        return (total / jnp.sqrt(square_mean + 1e-05) * norm_gain[None, :]).astype(jnp.bfloat16)
    result = lax.map(finish, (query_seg, key_seg, value_seg, decay_seg, first, docid, incoming))
    return result.reshape(WINDOW_TOKENS, width)
```

```python
import functools

import jax
import jax.numpy as jnp
from jax import lax
from jax.experimental import pallas as pl
from jax.experimental.pallas import tpu as pltpu
from jax.sharding import PartitionSpec as P

BLOCK = 128
MESH = pl.DeviceIdType.MESH
ORDER = (4, 2, 6, 1, 5, 3, 7)
ARRAYS = 3


def flipped(me, bits):
    high, mid, low = me // 4, (me // 2) % 2, me % 2
    return (
        4 * ((high + bits // 4) % 2) + 2 * ((mid + bits // 2 % 2) % 2) + (low + bits % 2) % 2
    )


def contract(a, b, dim_a, dim_b):
    return lax.dot_general(
        a, b, (((dim_a,), (dim_b,)), ((), ())), preferred_element_type=jnp.float32
    )


def attention_kernel(
    peers,
    q_hbm,
    k_hbm,
    v_hbm,
    log_ref,
    meta_ref,
    source_ref,
    out_hbm,
    total_ref,
    q_all,
    k_all,
    v_all,
    log_all,
    intra,
    own,
    gate,
    states,
    out_all,
    squares,
    squares_in,
    share_in,
    send_sem,
    recv_sem,
    log_send,
    log_recv,
    out_send,
    out_recv,
    sq_send,
    sq_recv,
    share_send,
    share_recv,
):
    ctx, head = peers
    me = lax.axis_index("ctx")
    plane = lax.axis_index("head")
    blocks = log_ref.shape[1]
    others = ORDER

    barrier = pltpu.get_barrier_semaphore()
    for bits in others:
        pl.semaphore_signal(
            barrier, inc=1, device_id=(flipped(me, bits), plane), device_id_type=MESH
        )
    for step in range(1, head):
        pl.semaphore_signal(
            barrier, inc=1, device_id=(me, (plane + step) % head), device_id_type=MESH
        )
    pl.semaphore_wait(barrier, ctx - 1 + head - 1)

    sources = (k_hbm, v_hbm, q_hbm)
    landings = (k_all, v_all, q_all)

    def columns(index):
        return pl.ds(pl.multiple_of(index * BLOCK, BLOCK), BLOCK)

    def span(index):
        return pl.ds(index * blocks, blocks)

    def log_copy(bits):
        there = flipped(me, bits)
        return pltpu.make_async_remote_copy(
            src_ref=log_ref.at[there],
            dst_ref=log_all.at[me],
            send_sem=log_send.at[bits],
            recv_sem=log_recv.at[bits],
            device_id=(there, plane),
            device_id_type=MESH,
        )

    def row_copy(bits, which):
        there = flipped(me, bits)
        return pltpu.make_async_remote_copy(
            src_ref=sources[which].at[:, :, columns(there)],
            dst_ref=landings[which].at[span(me)],
            send_sem=send_sem.at[bits, which],
            recv_sem=recv_sem.at[bits, which],
            device_id=(there, plane),
            device_id_type=MESH,
        )

    def row_landing(bits, which):
        there = flipped(me, bits)
        return pltpu.make_async_remote_copy(
            src_ref=sources[which].at[:, :, columns(there)],
            dst_ref=landings[which].at[span(there)],
            send_sem=send_sem.at[bits, which],
            recv_sem=recv_sem.at[bits, which],
            device_id=(there, plane),
            device_id_type=MESH,
        )

    def log_landing(bits):
        there = flipped(me, bits)
        return pltpu.make_async_remote_copy(
            src_ref=log_ref.at[there],
            dst_ref=log_all.at[there],
            send_sem=log_send.at[bits],
            recv_sem=log_recv.at[bits],
            device_id=(there, plane),
            device_id_type=MESH,
        )

    kept = [
        pltpu.make_async_copy(
            sources[which].at[:, :, columns(me)],
            landings[which].at[span(me)],
            recv_sem.at[0, which],
        )
        for which in range(ARRAYS)
    ]
    kept.append(pltpu.make_async_copy(log_ref.at[me], log_all.at[me], log_recv.at[0]))
    for copy in kept:
        copy.start()
    for bits in others:
        log_copy(bits).start()
    for bits in others:
        for which in range(ARRAYS):
            row_copy(bits, which).start()

    sub = lax.broadcasted_iota(jnp.int32, (BLOCK, BLOCK), 0)
    lane = lax.broadcasted_iota(jnp.int32, (BLOCK, BLOCK), 1)

    def local_block(there, index):
        log_row = log_all[there, pl.ds(index, 1), :]
        across = jnp.broadcast_to(log_row, (BLOCK, BLOCK))
        down = jnp.transpose(across)
        block = there * blocks + index
        begins = meta_ref[block, 0:1, :]
        broken_at = meta_ref[block, 1:2, :]
        last_begin = meta_ref[block, 2:3, :]
        queries = q_all[block]
        keys = k_all[block]
        values = v_all[block]
        scores = contract(keys, queries, 1, 1)
        allowed = (sub >= begins) & (sub <= lane)
        weight = jnp.where(allowed, jnp.exp(jnp.minimum(across - down, 0.0)), 0.0)
        weights = (scores * weight).astype(jnp.bfloat16)
        intra[block] = contract(weights, values, 0, 0)
        total = jnp.broadcast_to(log_row[:, BLOCK - 1 :], (1, BLOCK))
        keep = jnp.where(sub >= last_begin, jnp.exp(jnp.minimum(total - down, 0.0)), 0.0)
        decayed = (keys.astype(jnp.float32) * keep).astype(jnp.bfloat16)
        own[block] = contract(decayed, values, 0, 0)
        gate[block] = jnp.where(last_begin < 0, jnp.exp(total), 0.0)
        reach = jnp.where(sub < broken_at, jnp.exp(down), 0.0)
        q_all[block] = (queries.astype(jnp.float32) * reach).astype(jnp.bfloat16)

    def local_blocks(there):
        def several(step, carry):
            for extra in range(4):
                local_block(there, step * 4 + extra)
            return carry

        lax.fori_loop(0, blocks // 4, several, 0)

    for copy in kept:
        copy.wait()
    local_blocks(me)
    for bits in others:
        log_landing(bits).wait_recv()
        for which in range(ARRAYS):
            row_landing(bits, which).wait_recv()
        local_blocks(flipped(me, bits))

    def advance(step, state):
        for extra in range(4):
            place = step * 4 + extra
            block = source_ref[place]
            states[place] = state.astype(jnp.bfloat16)
            state = gate[block] * state + own[block]
        return state

    lax.fori_loop(0, ctx * blocks // 4, advance, jnp.zeros((BLOCK, BLOCK), jnp.float32))

    ones = jnp.ones((8, BLOCK), jnp.bfloat16)

    def out_copy(bits):
        there = flipped(me, bits)
        return pltpu.make_async_remote_copy(
            src_ref=out_all.at[span(there)],
            dst_ref=out_hbm.at[:, :, columns(me)],
            send_sem=out_send.at[bits],
            recv_sem=out_recv.at[bits],
            device_id=(there, plane),
            device_id_type=MESH,
        )

    def out_landing(bits):
        there = flipped(me, bits)
        return pltpu.make_async_remote_copy(
            src_ref=out_all.at[span(there)],
            dst_ref=out_hbm.at[:, :, columns(there)],
            send_sem=out_send.at[bits],
            recv_sem=out_recv.at[bits],
            device_id=(there, plane),
            device_id_type=MESH,
        )

    def sq_copy(bits):
        there = flipped(me, bits)
        return pltpu.make_async_remote_copy(
            src_ref=squares.at[there],
            dst_ref=squares_in.at[me],
            send_sem=sq_send.at[bits],
            recv_sem=sq_recv.at[bits],
            device_id=(there, plane),
            device_id_type=MESH,
        )

    def sq_landing(bits):
        there = flipped(me, bits)
        return pltpu.make_async_remote_copy(
            src_ref=squares.at[there],
            dst_ref=squares_in.at[there],
            send_sem=sq_send.at[bits],
            recv_sem=sq_recv.at[bits],
            device_id=(there, plane),
            device_id_type=MESH,
        )

    def finish(there):
        def several(step, carry):
            for extra in range(4):
                index = step * 4 + extra
                place = there * blocks + index
                block = source_ref[place]
                result = intra[block] + contract(q_all[block], states[place], 1, 0)
                out_all[place] = result.astype(jnp.bfloat16)
                summed = contract(ones, (result * result).astype(jnp.bfloat16), 1, 1)
                squares[there, pl.ds(index, 1), :] = summed[0:1]
            return carry

        lax.fori_loop(0, blocks // 4, several, 0)

    for bits in others:
        finish(flipped(me, bits))
        out_copy(bits).start()
        sq_copy(bits).start()
    finish(me)
    kept_out = pltpu.make_async_copy(
        out_all.at[span(me)], out_hbm.at[:, :, columns(me)], out_recv.at[0]
    )
    kept_out.start()
    summed = squares[me]
    for bits in others:
        sq_landing(bits).wait_recv()
        summed = summed + squares_in[flipped(me, bits)]
    share_in[plane] = summed

    def share_copy(step, slot):
        return pltpu.make_async_remote_copy(
            src_ref=share_in.at[plane],
            dst_ref=share_in.at[slot],
            send_sem=share_send.at[step],
            recv_sem=share_recv.at[step],
            device_id=(me, (plane + step) % head),
            device_id_type=MESH,
        )

    for step in range(1, head):
        share_copy(step, plane).start()
    total = summed
    for step in range(1, head):
        origin = (plane + head - step) % head
        share_copy(step, origin).wait_recv()
        total = total + share_in[origin]
    total_ref[...] = total
    kept_out.wait()
    for bits in others:
        out_landing(bits).wait_recv()
    for bits in others:
        log_copy(bits).wait_send()
        for which in range(ARRAYS):
            row_copy(bits, which).wait_send()
        out_copy(bits).wait_send()
        sq_copy(bits).wait_send()
    for step in range(1, head):
        share_copy(step, plane).wait_send()


def by_head(queries, key_rows, value_rows, log_decay, norm_gain, doc_lengths, packing):
    rows, width = queries.shape
    heads = log_decay.shape[1]
    blocks = rows // BLOCK
    ctx = lax.axis_size("ctx")
    head = lax.axis_size("head")
    total_blocks = packing.shape[0]

    order = jnp.arange(BLOCK)
    lower = (order[:, None] >= order[None, :]).astype(jnp.bfloat16)
    logs = jnp.einsum(
        "ts,nsh->hnt",
        lower,
        log_decay.reshape(blocks, BLOCK, heads),
        preferred_element_type=jnp.float32,
    )
    starts = jnp.cumsum(doc_lengths) - doc_lengths
    base = packing * BLOCK
    relative = starts[None, None, :] - base[:, None, None]
    begins = jnp.max(jnp.where(relative <= order[None, :, None], relative, -(1 << 24)), axis=2)
    broken_at = jnp.min(jnp.where(relative >= 0, relative, BLOCK), axis=2)
    broken_at = jnp.broadcast_to(broken_at, begins.shape)
    last_begin = jnp.broadcast_to(begins[:, -1:], begins.shape)
    meta = jnp.stack([begins, broken_at, last_begin], axis=1)
    places = jnp.arange(total_blocks, dtype=jnp.int32)
    source = jnp.sum(
        jnp.where(packing[None, :] == places[:, None], places[None, :], 0), axis=1
    ).astype(jnp.int32)

    def in_blocks(values):
        return values.reshape(blocks, BLOCK, width)

    any_spec = pl.BlockSpec(memory_space=pl.ANY)
    vmem = pl.BlockSpec(memory_space=pltpu.VMEM)
    dma = pltpu.SemaphoreType.DMA
    out, squares = pl.pallas_call(
        functools.partial(attention_kernel, (ctx, head)),
        out_shape=(
            jax.ShapeDtypeStruct((blocks, BLOCK, width), jnp.bfloat16),
            jax.ShapeDtypeStruct((blocks, BLOCK), jnp.float32),
        ),
        in_specs=[any_spec] * 3 + [vmem, vmem, pl.BlockSpec(memory_space=pltpu.SMEM)],
        out_specs=(any_spec, vmem),
        scratch_shapes=[
            pltpu.VMEM((total_blocks, BLOCK, BLOCK), jnp.bfloat16),
            pltpu.VMEM((total_blocks, BLOCK, BLOCK), jnp.bfloat16),
            pltpu.VMEM((total_blocks, BLOCK, BLOCK), jnp.bfloat16),
            pltpu.VMEM((ctx, blocks, BLOCK), jnp.float32),
            pltpu.VMEM((total_blocks, BLOCK, BLOCK), jnp.float32),
            pltpu.VMEM((total_blocks, BLOCK, BLOCK), jnp.float32),
            pltpu.VMEM((total_blocks, 1, BLOCK), jnp.float32),
            pltpu.VMEM((total_blocks, BLOCK, BLOCK), jnp.bfloat16),
            pltpu.VMEM((total_blocks, BLOCK, BLOCK), jnp.bfloat16),
            pltpu.VMEM((ctx, blocks, BLOCK), jnp.float32),
            pltpu.VMEM((ctx, blocks, BLOCK), jnp.float32),
            pltpu.VMEM((head, blocks, BLOCK), jnp.float32),
            dma((ctx, ARRAYS)),
            dma((ctx, ARRAYS)),
            dma((ctx,)),
            dma((ctx,)),
            dma((ctx,)),
            dma((ctx,)),
            dma((ctx,)),
            dma((ctx,)),
            dma((head,)),
            dma((head,)),
        ],
        compiler_params=pltpu.CompilerParams(
            collective_id=0, has_side_effects=True, vmem_limit_bytes=52 * 1024 * 1024
        ),
        name="attention_by_head",
    )(in_blocks(queries), in_blocks(key_rows), in_blocks(value_rows), logs, meta, source)
    scale = lax.rsqrt(squares / (width * head) + 1e-05)
    normed = out.astype(jnp.float32) * scale[:, :, None] * norm_gain[None, None, :]
    return normed.astype(jnp.bfloat16).reshape(rows, width)


def from_behind(x, axis, by):
    count = lax.axis_size(axis)
    pairs = [(i, i + by) for i in range(count) if 0 <= i + by < count]
    return lax.ppermute(x, axis, pairs)


def state_pass(key_blocks, value_blocks, decay_blocks, first, docid):
    block_log = jnp.cumsum(decay_blocks.astype(jnp.float32), axis=1)
    block_total = block_log[:, -1, :]
    seen = jnp.cumsum(first, axis=1)
    reach_block = (seen == 0).astype(jnp.float32)
    unbroken = (seen[:, -1] == 0).astype(jnp.float32)
    same_last = (docid == docid[:, -1:]).astype(jnp.float32)
    keep = jnp.exp(block_total[:, None, :] - block_log) * same_last[:, :, None]
    key_decayed = (key_blocks.astype(jnp.float32) * keep[..., None]).astype(jnp.bfloat16)
    own = jnp.einsum(
        "nshd,nshe->nhde", key_decayed, value_blocks, preferred_element_type=jnp.float32
    )
    gate = jnp.exp(block_total) * unbroken[:, None]

    def advance(state, item):
        factor, term = item
        return (factor[:, None, None] * state + term, state)

    start = jnp.zeros(own.shape[1:], jnp.float32)
    s_end, states = lax.scan(advance, start, (gate, own))
    prior = jnp.cumsum(block_total, axis=0) - block_total
    segment_log = block_log + prior[:, None, :]
    block_starts = seen[:, -1]
    before = jnp.cumsum(block_starts) - block_starts
    reach_segment = (seen + before[:, None] == 0).astype(jnp.float32)
    clean = (jnp.sum(first) == 0).astype(jnp.float32)
    decay_all = jnp.exp(segment_log[-1, -1]) * clean
    return (block_log, reach_block, states, segment_log, reach_segment, decay_all, s_end)


def query_pass(query_blocks, key_blocks, value_blocks, block_log, reach_block, states, docid):
    length = docid.shape[1]
    order = jnp.arange(length)
    causal = order[:, None] >= order[None, :]
    allowed = causal[None] & (docid[:, :, None] == docid[:, None, :])
    by_head = jnp.transpose(block_log, (0, 2, 1))
    gaps = by_head[:, :, :, None] - by_head[:, :, None, :]
    weight = jnp.where(allowed[:, None], jnp.exp(jnp.minimum(gaps, 0.0)), 0.0)
    scores = jnp.einsum(
        "nthd,nshd->nhts", query_blocks, key_blocks, preferred_element_type=jnp.float32
    )
    weights = (scores * weight).astype(jnp.bfloat16)
    intra = jnp.einsum("nhts,nshd->nthd", weights, value_blocks, preferred_element_type=jnp.float32)
    query_decayed = (
        query_blocks.astype(jnp.float32) * (jnp.exp(block_log) * reach_block[:, :, None])[..., None]
    ).astype(jnp.bfloat16)
    inter = jnp.einsum(
        "nthd,nhde->nthe",
        query_decayed,
        states.astype(jnp.bfloat16),
        preferred_element_type=jnp.float32,
    )
    return intra + inter


def carry_in(decay_all, s_end, devices):
    zero_state = jnp.zeros(s_end.shape, jnp.float32)

    def forward(index, pair):
        arrived = from_behind(pair[1], "ctx", 1)
        return (arrived, decay_all[:, None, None] * arrived + s_end)

    arrival, leaving = lax.fori_loop(0, devices - 1, forward, (zero_state, s_end))
    return arrival


def body(queries, key_rows, value_rows, log_decay, norm_gain, doc_lengths, packing):
    rows, width = queries.shape
    heads = log_decay.shape[1]
    head_size = width // heads
    blocks = rows // BLOCK
    devices = lax.axis_size("ctx")
    mine = lax.axis_index("ctx")
    total_blocks = packing.shape[0]
    capacity = (2 * blocks + devices - 1) // devices
    owners = (packing // blocks).reshape(devices, blocks)
    local = jnp.arange(blocks, dtype=jnp.int32)
    earlier_mask = local[:, None] < local[None, :]
    same_owner = owners[:, :, None] == owners[:, None, :]
    ranks = jnp.sum((same_owner & earlier_mask[None]).astype(jnp.int32), axis=1)
    my_owner = lax.dynamic_index_in_dim(owners, mine, 0, keepdims=False)
    my_rank = lax.dynamic_index_in_dim(ranks, mine, 0, keepdims=False)
    slot_of = my_owner * capacity + my_rank
    slot_ids = jnp.arange(devices * capacity, dtype=jnp.int32)
    matched = slot_of[None, :] == slot_ids[:, None]
    source = jnp.sum(matched.astype(jnp.int32) * local[None, :], axis=1)
    filled = jnp.any(matched, axis=1)

    def outgoing(values):
        columns = values.shape[1]
        picked = jnp.take(values.reshape(blocks, BLOCK, columns), source, axis=0)
        kept = jnp.where(filled[:, None, None], picked, jnp.zeros((), values.dtype))
        return kept.reshape(devices, capacity * BLOCK, columns)

    target = mine * blocks + local
    block_index = jnp.arange(total_blocks, dtype=jnp.int32)
    wanted = packing[None, :] == target[:, None]
    loader_block = jnp.sum(wanted.astype(jnp.int32) * block_index[None, :], axis=1)
    column = loader_block // blocks * capacity + jnp.take(ranks.reshape(-1), loader_block)

    def arriving(values):
        return jnp.take(values.reshape(devices * capacity, BLOCK, values.shape[2]), column, axis=0)

    starts = jnp.cumsum(doc_lengths) - doc_lengths
    positions = mine * rows + jnp.arange(rows, dtype=jnp.int32)
    first = (
        jnp.any(positions[:, None] == starts[None, :], axis=1)
        .astype(jnp.int32)
        .reshape(blocks, BLOCK)
    )
    docid = (
        jnp.sum((starts[None, :] <= positions[:, None]).astype(jnp.int32), axis=1) - 1
    ).reshape(blocks, BLOCK)
    got_queries, got_keys, got_values, received_decay = (
        lax.all_to_all(outgoing(queries), "ctx", split_axis=0, concat_axis=0, tiled=True),
        lax.all_to_all(outgoing(key_rows), "ctx", split_axis=0, concat_axis=0, tiled=True),
        lax.all_to_all(outgoing(value_rows), "ctx", split_axis=0, concat_axis=0, tiled=True),
        lax.all_to_all(outgoing(log_decay), "ctx", split_axis=0, concat_axis=0, tiled=True),
    )
    key_blocks = arriving(got_keys).reshape(blocks, BLOCK, heads, head_size)
    value_blocks = arriving(got_values).reshape(blocks, BLOCK, heads, head_size)
    decay_blocks = arriving(received_decay)
    block_log, reach_block, states, segment_log, reach_segment, decay_all, s_end = state_pass(
        key_blocks, value_blocks, decay_blocks, first, docid
    )
    arrival = carry_in(decay_all, s_end, devices)
    query_blocks = arriving(got_queries).reshape(blocks, BLOCK, heads, head_size)
    local_out = query_pass(
        query_blocks, key_blocks, value_blocks, block_log, reach_block, states, docid
    )
    scaled = (
        query_blocks.astype(jnp.float32)
        * (jnp.exp(segment_log) * reach_segment[:, :, None])[..., None]
    ).astype(jnp.bfloat16)
    carried = jnp.einsum(
        "nthd,hde->nthe", scaled, arrival.astype(jnp.bfloat16), preferred_element_type=jnp.float32
    )
    total = (local_out + carried).reshape(rows, width)
    squares = lax.psum(jnp.sum(total * total, axis=1), "head")
    columns_all = width * lax.axis_size("head")
    scale = lax.rsqrt(squares / columns_all + 1e-05)
    return (total * scale[:, None] * norm_gain[None, :]).astype(jnp.bfloat16)


def solution(mesh):
    placed = (
        P("ctx", "head"),
        P("ctx", "head"),
        P("ctx", "head"),
        P("ctx", "head"),
        P("head"),
        P(),
        P(),
    )
    one_head_each = mesh.shape["ctx"] == 8 and mesh.shape["head"] == 4
    return jax.shard_map(
        by_head if one_head_each else body, mesh=mesh, in_specs=placed, out_specs=P("ctx", "head"), check_vma=False
    )
```

```python
import functools

import jax
import jax.numpy as jnp
from jax import lax
from jax.experimental import pallas as pl
from jax.experimental.pallas import tpu as pltpu
from jax.sharding import PartitionSpec as P

BLOCK = 128
MESH = pl.DeviceIdType.MESH
ORDER = (4, 2, 6, 1, 5, 3, 7)
ARRAYS = 3
AHEAD = 2


def stage_list(blocks):
    stages = []
    slot = 0
    for low in range(0, blocks, 4):
        stages.append(((0, 1), low, 4, slot))
        slot += 2
    for low in range(0, blocks, 2):
        stages.append(((2,), low, 2, slot))
        slot += 1
    return stages


def flipped(me, bits):
    high, mid, low = me // 4, (me // 2) % 2, me % 2
    return (
        4 * ((high + bits // 4) % 2) + 2 * ((mid + bits // 2 % 2) % 2) + (low + bits % 2) % 2
    )


def contract(a, b, dim_a, dim_b):
    return lax.dot_general(
        a, b, (((dim_a,), (dim_b,)), ((), ())), preferred_element_type=jnp.float32
    )


def attention_kernel(
    peers,
    q_hbm,
    k_hbm,
    v_hbm,
    log_ref,
    length_ref,
    packing_ref,
    source_ref,
    out_hbm,
    total_ref,
    q_all,
    k_all,
    v_all,
    log_all,
    meta,
    intra,
    own,
    gate,
    states,
    out_all,
    squares,
    squares_in,
    share_in,
    send_sem,
    recv_sem,
    kept_sem,
    log_send,
    log_recv,
    out_send,
    out_recv,
    sq_send,
    sq_recv,
    share_send,
    share_recv,
):
    ctx, head = peers
    me = lax.axis_index("ctx")
    plane = lax.axis_index("head")
    blocks = log_ref.shape[1]
    total_blocks = ctx * blocks
    others = ORDER

    barrier = pltpu.get_barrier_semaphore()
    for bits in others:
        pl.semaphore_signal(
            barrier, inc=1, device_id=(flipped(me, bits), plane), device_id_type=MESH
        )
    for step in range(1, head):
        pl.semaphore_signal(
            barrier, inc=1, device_id=(me, (plane + step) % head), device_id_type=MESH
        )
    pl.semaphore_wait(barrier, ctx - 1 + head - 1)

    pairs = ((k_hbm, k_all), (v_hbm, v_all), (q_hbm, q_all))
    stages = stage_list(blocks)

    def columns(index):
        return pl.ds(pl.multiple_of(index * BLOCK, BLOCK), BLOCK)

    def span(index, low=0, count=blocks):
        return pl.ds(index * blocks + low, count)

    def remote(source, target, send, recv, there):
        return pltpu.make_async_remote_copy(
            src_ref=source,
            dst_ref=target,
            send_sem=send,
            recv_sem=recv,
            device_id=(there, plane),
            device_id_type=MESH,
        )

    def row_copies(stage, bits, arriving):
        arrays, low, count, slot = stages[stage]
        there = flipped(me, bits)
        origin = there if arriving else me
        return [
            remote(
                pairs[which][0].at[pl.ds(low, count), :, columns(there)],
                pairs[which][1].at[span(origin, low, count)],
                send_sem.at[slot + extra, bits],
                recv_sem.at[slot + extra, bits],
                there,
            )
            for extra, which in enumerate(arrays)
        ]

    def log_copy(bits, arriving):
        there = flipped(me, bits)
        origin = there if arriving else me
        return remote(
            log_ref.at[there], log_all.at[origin], log_send.at[bits], log_recv.at[bits], there
        )

    def begin(stage):
        for bits in others:
            for copy in row_copies(stage, bits, False):
                copy.start()

    def sent(stage):
        for bits in others:
            for copy in row_copies(stage, bits, False):
                copy.wait_send()

    def arrived(stage):
        for bits in others:
            for copy in row_copies(stage, bits, True):
                copy.wait_recv()

    for bits in others:
        log_copy(bits, False).start()
    for stage in range(AHEAD):
        begin(stage)
    kept = [
        pltpu.make_async_copy(
            source.at[:, :, columns(me)], landing.at[span(me)], kept_sem.at[index]
        )
        for index, (source, landing) in enumerate(pairs)
    ]
    kept.append(pltpu.make_async_copy(log_ref.at[me], log_all.at[me], kept_sem.at[ARRAYS]))
    for copy in kept:
        copy.start()

    sub = lax.broadcasted_iota(jnp.int32, (BLOCK, BLOCK), 0)
    lane = lax.broadcasted_iota(jnp.int32, (BLOCK, BLOCK), 1)
    along = lax.broadcasted_iota(jnp.int32, (1, BLOCK), 1)

    starts = [jnp.int32(0)]
    for index in range(length_ref.shape[0] - 1):
        starts.append(starts[-1] + length_ref[index])

    def mark(block, carry):
        base = packing_ref[block] * BLOCK
        begins = jnp.full((1, BLOCK), -(1 << 24), jnp.int32)
        broken_at = jnp.full((1, BLOCK), BLOCK, jnp.int32)
        for start in starts:
            relative = jnp.broadcast_to(start - base, (1, BLOCK))
            begins = jnp.maximum(begins, jnp.where(relative <= along, relative, -(1 << 24)))
            broken_at = jnp.minimum(broken_at, jnp.where(relative >= 0, relative, BLOCK))
        meta[block, 0:1, :] = begins
        meta[block, 1:2, :] = broken_at
        meta[block, 2:3, :] = jnp.broadcast_to(begins[:, BLOCK - 1 :], (1, BLOCK))
        return carry

    lax.fori_loop(0, total_blocks, mark, 0)
    for copy in kept:
        copy.wait()
    for bits in others:
        log_copy(bits, True).wait_recv()

    def down(row):
        return jnp.transpose(jnp.broadcast_to(row, (BLOCK, BLOCK)))

    def key_block(there, index):
        block = there * blocks + index
        log_row = log_all[there, index : index + 1, :]
        last_begin = meta[block, 2:3, :]
        total = jnp.broadcast_to(log_row[:, BLOCK - 1 :], (1, BLOCK))
        keep = jnp.where(along >= last_begin, jnp.exp(total - log_row), 0.0)
        decayed = (k_all[block].astype(jnp.float32) * down(keep)).astype(jnp.bfloat16)
        own[block] = contract(decayed, v_all[block], 0, 0)
        gate[block] = jnp.where(last_begin < 0, jnp.exp(total), 0.0)

    def query_block(there, index):
        block = there * blocks + index
        log_row = log_all[there, index : index + 1, :]
        begins = meta[block, 0:1, :]
        broken_at = meta[block, 1:2, :]
        queries = q_all[block]
        scores = contract(k_all[block], queries, 1, 1)
        allowed = (sub >= begins) & (sub <= lane)
        gaps = jnp.minimum(log_row - down(log_row), 0.0)
        weights = jnp.where(allowed, scores * jnp.exp(gaps), 0.0).astype(jnp.bfloat16)
        intra[block] = contract(weights, v_all[block], 0, 0)
        reach = jnp.where(along < broken_at, jnp.exp(log_row), 0.0)
        q_all[block] = (queries.astype(jnp.float32) * down(reach)).astype(jnp.bfloat16)

    def work(stage):
        arrays, low, count, slot = stages[stage]
        each = key_block if len(arrays) > 1 else query_block
        at_once = max(1, 4 // count)

        def several(step, carry):
            for extra in range(at_once):
                for index in range(low, low + count):
                    each(step * at_once + extra, index)
            return carry

        lax.fori_loop(0, ctx // at_once, several, 0)

    def advance(step, state):
        for extra in range(4):
            place = step * 4 + extra
            block = source_ref[place]
            states[place] = state.astype(jnp.bfloat16)
            state = gate[block] * state + own[block]
        return state

    for stage in range(len(stages)):
        arrived(stage)
        if stage + AHEAD < len(stages):
            sent(stage)
            begin(stage + AHEAD)
        work(stage)
        if stage + 1 < len(stages) and len(stages[stage][0]) > len(stages[stage + 1][0]):
            zero_state = jnp.zeros((BLOCK, BLOCK), jnp.float32)
            lax.fori_loop(0, total_blocks // 4, advance, zero_state)

    ones = jnp.ones((8, BLOCK), jnp.bfloat16)

    def out_copy(bits, arriving):
        there = flipped(me, bits)
        origin = there if arriving else me
        return remote(
            out_all.at[span(there)],
            out_hbm.at[:, :, columns(origin)],
            out_send.at[bits],
            out_recv.at[bits],
            there,
        )

    def sq_copy(bits, arriving):
        there = flipped(me, bits)
        origin = there if arriving else me
        return remote(
            squares.at[there], squares_in.at[origin], sq_send.at[bits], sq_recv.at[bits], there
        )

    def finish(there):
        def several(step, carry):
            for extra in range(4):
                index = step * 4 + extra
                place = there * blocks + index
                block = source_ref[place]
                result = intra[block] + contract(q_all[block], states[place], 1, 0)
                out_all[place] = result.astype(jnp.bfloat16)
                summed = contract(ones, (result * result).astype(jnp.bfloat16), 1, 1)
                squares[there, pl.ds(index, 1), :] = summed[0:1]
            return carry

        lax.fori_loop(0, blocks // 4, several, 0)

    held_back = others[4:]
    for bits in others:
        finish(flipped(me, bits))
        if bits not in held_back:
            out_copy(bits, False).start()
    for bits in others:
        sq_copy(bits, False).start()
    for bits in held_back:
        out_copy(bits, False).start()
    finish(me)
    kept_out = pltpu.make_async_copy(
        out_all.at[span(me)], out_hbm.at[:, :, columns(me)], kept_sem.at[0]
    )
    kept_out.start()
    summed = squares[me]
    for bits in others:
        sq_copy(bits, True).wait_recv()
        summed = summed + squares_in[flipped(me, bits)]
    share_in[plane] = summed

    def share_copy(step, slot):
        return pltpu.make_async_remote_copy(
            src_ref=share_in.at[plane],
            dst_ref=share_in.at[slot],
            send_sem=share_send.at[step],
            recv_sem=share_recv.at[step],
            device_id=(me, (plane + step) % head),
            device_id_type=MESH,
        )

    for step in range(1, head):
        share_copy(step, plane).start()
    total = summed
    for step in range(1, head):
        origin = (plane + head - step) % head
        share_copy(step, origin).wait_recv()
        total = total + share_in[origin]
    total_ref[...] = total
    for stage in range(len(stages) - AHEAD, len(stages)):
        sent(stage)
    kept_out.wait()
    for bits in others:
        out_copy(bits, True).wait_recv()
    for bits in others:
        log_copy(bits, False).wait_send()
        out_copy(bits, False).wait_send()
        sq_copy(bits, False).wait_send()
    for step in range(1, head):
        share_copy(step, plane).wait_send()


def by_head(queries, key_rows, value_rows, log_decay, norm_gain, doc_lengths, packing):
    rows, width = queries.shape
    heads = log_decay.shape[1]
    blocks = rows // BLOCK
    ctx = lax.axis_size("ctx")
    head = lax.axis_size("head")
    total_blocks = packing.shape[0]

    order = jnp.arange(BLOCK)
    lower = (order[:, None] >= order[None, :]).astype(jnp.bfloat16)
    logs = jnp.einsum(
        "ts,nsh->hnt",
        lower,
        log_decay.reshape(blocks, BLOCK, heads),
        preferred_element_type=jnp.float32,
    )
    places = jnp.arange(total_blocks, dtype=jnp.int32)
    source = jnp.sum(
        jnp.where(packing[None, :] == places[:, None], places[None, :], 0), axis=1
    ).astype(jnp.int32)

    def in_blocks(values):
        return values.reshape(blocks, BLOCK, width)

    copies = sum(len(stage[0]) for stage in stage_list(blocks))
    any_spec = pl.BlockSpec(memory_space=pl.ANY)
    vmem = pl.BlockSpec(memory_space=pltpu.VMEM)
    dma = pltpu.SemaphoreType.DMA
    out, squares = pl.pallas_call(
        functools.partial(attention_kernel, (ctx, head)),
        out_shape=(
            jax.ShapeDtypeStruct((blocks, BLOCK, width), jnp.bfloat16),
            jax.ShapeDtypeStruct((blocks, BLOCK), jnp.float32),
        ),
        in_specs=[any_spec] * 3 + [vmem] + [pl.BlockSpec(memory_space=pltpu.SMEM)] * 3,
        out_specs=(any_spec, vmem),
        scratch_shapes=[
            pltpu.VMEM((total_blocks, BLOCK, BLOCK), jnp.bfloat16),
            pltpu.VMEM((total_blocks, BLOCK, BLOCK), jnp.bfloat16),
            pltpu.VMEM((total_blocks, BLOCK, BLOCK), jnp.bfloat16),
            pltpu.VMEM((ctx, blocks, BLOCK), jnp.float32),
            pltpu.VMEM((total_blocks, 8, BLOCK), jnp.int32),
            pltpu.VMEM((total_blocks, BLOCK, BLOCK), jnp.float32),
            pltpu.VMEM((total_blocks, BLOCK, BLOCK), jnp.float32),
            pltpu.VMEM((total_blocks, 1, BLOCK), jnp.float32),
            pltpu.VMEM((total_blocks, BLOCK, BLOCK), jnp.bfloat16),
            pltpu.VMEM((total_blocks, BLOCK, BLOCK), jnp.bfloat16),
            pltpu.VMEM((ctx, blocks, BLOCK), jnp.float32),
            pltpu.VMEM((ctx, blocks, BLOCK), jnp.float32),
            pltpu.VMEM((head, blocks, BLOCK), jnp.float32),
            dma((copies, ctx)),
            dma((copies, ctx)),
            dma((ARRAYS + 1,)),
            dma((ctx,)),
            dma((ctx,)),
            dma((ctx,)),
            dma((ctx,)),
            dma((ctx,)),
            dma((ctx,)),
            dma((head,)),
            dma((head,)),
        ],
        compiler_params=pltpu.CompilerParams(
            collective_id=0, has_side_effects=True, vmem_limit_bytes=52 * 1024 * 1024
        ),
        name="attention_by_head",
    )(in_blocks(queries), in_blocks(key_rows), in_blocks(value_rows), logs, doc_lengths, packing, source)
    scale = lax.rsqrt(squares / (width * head) + 1e-05)
    normed = out.astype(jnp.float32) * scale[:, :, None] * norm_gain[None, None, :]
    return normed.astype(jnp.bfloat16).reshape(rows, width)


def from_behind(x, axis, by):
    count = lax.axis_size(axis)
    pairs = [(i, i + by) for i in range(count) if 0 <= i + by < count]
    return lax.ppermute(x, axis, pairs)


def state_pass(key_blocks, value_blocks, decay_blocks, first, docid):
    block_log = jnp.cumsum(decay_blocks.astype(jnp.float32), axis=1)
    block_total = block_log[:, -1, :]
    seen = jnp.cumsum(first, axis=1)
    reach_block = (seen == 0).astype(jnp.float32)
    unbroken = (seen[:, -1] == 0).astype(jnp.float32)
    same_last = (docid == docid[:, -1:]).astype(jnp.float32)
    keep = jnp.exp(block_total[:, None, :] - block_log) * same_last[:, :, None]
    key_decayed = (key_blocks.astype(jnp.float32) * keep[..., None]).astype(jnp.bfloat16)
    own = jnp.einsum(
        "nshd,nshe->nhde", key_decayed, value_blocks, preferred_element_type=jnp.float32
    )
    gate = jnp.exp(block_total) * unbroken[:, None]

    def advance(state, item):
        factor, term = item
        return (factor[:, None, None] * state + term, state)

    start = jnp.zeros(own.shape[1:], jnp.float32)
    s_end, states = lax.scan(advance, start, (gate, own))
    prior = jnp.cumsum(block_total, axis=0) - block_total
    segment_log = block_log + prior[:, None, :]
    block_starts = seen[:, -1]
    before = jnp.cumsum(block_starts) - block_starts
    reach_segment = (seen + before[:, None] == 0).astype(jnp.float32)
    clean = (jnp.sum(first) == 0).astype(jnp.float32)
    decay_all = jnp.exp(segment_log[-1, -1]) * clean
    return (block_log, reach_block, states, segment_log, reach_segment, decay_all, s_end)


def query_pass(query_blocks, key_blocks, value_blocks, block_log, reach_block, states, docid):
    length = docid.shape[1]
    order = jnp.arange(length)
    causal = order[:, None] >= order[None, :]
    allowed = causal[None] & (docid[:, :, None] == docid[:, None, :])
    by_head = jnp.transpose(block_log, (0, 2, 1))
    gaps = by_head[:, :, :, None] - by_head[:, :, None, :]
    weight = jnp.where(allowed[:, None], jnp.exp(jnp.minimum(gaps, 0.0)), 0.0)
    scores = jnp.einsum(
        "nthd,nshd->nhts", query_blocks, key_blocks, preferred_element_type=jnp.float32
    )
    weights = (scores * weight).astype(jnp.bfloat16)
    intra = jnp.einsum("nhts,nshd->nthd", weights, value_blocks, preferred_element_type=jnp.float32)
    query_decayed = (
        query_blocks.astype(jnp.float32) * (jnp.exp(block_log) * reach_block[:, :, None])[..., None]
    ).astype(jnp.bfloat16)
    inter = jnp.einsum(
        "nthd,nhde->nthe",
        query_decayed,
        states.astype(jnp.bfloat16),
        preferred_element_type=jnp.float32,
    )
    return intra + inter


def carry_in(decay_all, s_end, devices):
    zero_state = jnp.zeros(s_end.shape, jnp.float32)

    def forward(index, pair):
        arrived = from_behind(pair[1], "ctx", 1)
        return (arrived, decay_all[:, None, None] * arrived + s_end)

    arrival, leaving = lax.fori_loop(0, devices - 1, forward, (zero_state, s_end))
    return arrival


def body(queries, key_rows, value_rows, log_decay, norm_gain, doc_lengths, packing):
    rows, width = queries.shape
    heads = log_decay.shape[1]
    head_size = width // heads
    blocks = rows // BLOCK
    devices = lax.axis_size("ctx")
    mine = lax.axis_index("ctx")
    total_blocks = packing.shape[0]
    capacity = (2 * blocks + devices - 1) // devices
    owners = (packing // blocks).reshape(devices, blocks)
    local = jnp.arange(blocks, dtype=jnp.int32)
    earlier_mask = local[:, None] < local[None, :]
    same_owner = owners[:, :, None] == owners[:, None, :]
    ranks = jnp.sum((same_owner & earlier_mask[None]).astype(jnp.int32), axis=1)
    my_owner = lax.dynamic_index_in_dim(owners, mine, 0, keepdims=False)
    my_rank = lax.dynamic_index_in_dim(ranks, mine, 0, keepdims=False)
    slot_of = my_owner * capacity + my_rank
    slot_ids = jnp.arange(devices * capacity, dtype=jnp.int32)
    matched = slot_of[None, :] == slot_ids[:, None]
    source = jnp.sum(matched.astype(jnp.int32) * local[None, :], axis=1)
    filled = jnp.any(matched, axis=1)

    def outgoing(values):
        columns = values.shape[1]
        picked = jnp.take(values.reshape(blocks, BLOCK, columns), source, axis=0)
        kept = jnp.where(filled[:, None, None], picked, jnp.zeros((), values.dtype))
        return kept.reshape(devices, capacity * BLOCK, columns)

    target = mine * blocks + local
    block_index = jnp.arange(total_blocks, dtype=jnp.int32)
    wanted = packing[None, :] == target[:, None]
    loader_block = jnp.sum(wanted.astype(jnp.int32) * block_index[None, :], axis=1)
    column = loader_block // blocks * capacity + jnp.take(ranks.reshape(-1), loader_block)

    def arriving(values):
        return jnp.take(values.reshape(devices * capacity, BLOCK, values.shape[2]), column, axis=0)

    starts = jnp.cumsum(doc_lengths) - doc_lengths
    positions = mine * rows + jnp.arange(rows, dtype=jnp.int32)
    first = (
        jnp.any(positions[:, None] == starts[None, :], axis=1)
        .astype(jnp.int32)
        .reshape(blocks, BLOCK)
    )
    docid = (
        jnp.sum((starts[None, :] <= positions[:, None]).astype(jnp.int32), axis=1) - 1
    ).reshape(blocks, BLOCK)
    got_queries, got_keys, got_values, received_decay = (
        lax.all_to_all(outgoing(queries), "ctx", split_axis=0, concat_axis=0, tiled=True),
        lax.all_to_all(outgoing(key_rows), "ctx", split_axis=0, concat_axis=0, tiled=True),
        lax.all_to_all(outgoing(value_rows), "ctx", split_axis=0, concat_axis=0, tiled=True),
        lax.all_to_all(outgoing(log_decay), "ctx", split_axis=0, concat_axis=0, tiled=True),
    )
    key_blocks = arriving(got_keys).reshape(blocks, BLOCK, heads, head_size)
    value_blocks = arriving(got_values).reshape(blocks, BLOCK, heads, head_size)
    decay_blocks = arriving(received_decay)
    block_log, reach_block, states, segment_log, reach_segment, decay_all, s_end = state_pass(
        key_blocks, value_blocks, decay_blocks, first, docid
    )
    arrival = carry_in(decay_all, s_end, devices)
    query_blocks = arriving(got_queries).reshape(blocks, BLOCK, heads, head_size)
    local_out = query_pass(
        query_blocks, key_blocks, value_blocks, block_log, reach_block, states, docid
    )
    scaled = (
        query_blocks.astype(jnp.float32)
        * (jnp.exp(segment_log) * reach_segment[:, :, None])[..., None]
    ).astype(jnp.bfloat16)
    carried = jnp.einsum(
        "nthd,hde->nthe", scaled, arrival.astype(jnp.bfloat16), preferred_element_type=jnp.float32
    )
    total = (local_out + carried).reshape(rows, width)
    squares = lax.psum(jnp.sum(total * total, axis=1), "head")
    columns_all = width * lax.axis_size("head")
    scale = lax.rsqrt(squares / columns_all + 1e-05)
    return (total * scale[:, None] * norm_gain[None, :]).astype(jnp.bfloat16)


def solution(mesh):
    placed = (
        P("ctx", "head"),
        P("ctx", "head"),
        P("ctx", "head"),
        P("ctx", "head"),
        P("head"),
        P(),
        P(),
    )
    one_head_each = mesh.shape["ctx"] == 8 and mesh.shape["head"] == 4
    return jax.shard_map(
        by_head if one_head_each else body, mesh=mesh, in_specs=placed, out_specs=P("ctx", "head"), check_vma=False
    )
```

```python
import functools

import jax
import jax.numpy as jnp
from jax import lax
from jax.experimental import pallas as pl
from jax.experimental.pallas import tpu as pltpu
from jax.sharding import PartitionSpec as P

BLOCK = 128
MESH = pl.DeviceIdType.MESH
ORDER = (4, 2, 5, 3, 6, 7, 1)
ARRAYS = 3
AHEAD = 2


def stage_list(blocks):
    stages = []
    slot = 0
    for low in range(0, blocks, 4):
        stages.append(((0, 1), low, 4, slot))
        slot += 2
    for low in range(0, blocks, 2):
        stages.append(((2,), low, 2, slot))
        slot += 1
    return stages


def flipped(me, bits):
    high, mid, low = me // 4, (me // 2) % 2, me % 2
    return (
        4 * ((high + bits // 4) % 2) + 2 * ((mid + bits // 2 % 2) % 2) + (low + bits % 2) % 2
    )


def turned(me, bits):
    swapped = 4 * (bits // 2 % 2) + 2 * (bits // 4) + bits % 2
    return bits + (swapped - bits) * (me % 2)


def contract(a, b, dim_a, dim_b):
    return lax.dot_general(
        a, b, (((dim_a,), (dim_b,)), ((), ())), preferred_element_type=jnp.float32
    )


def attention_kernel(
    peers,
    q_hbm,
    k_hbm,
    v_hbm,
    log_ref,
    length_ref,
    packing_ref,
    source_ref,
    out_hbm,
    total_ref,
    q_all,
    k_all,
    v_all,
    log_all,
    meta,
    intra,
    own,
    gate,
    states,
    out_all,
    squares,
    squares_in,
    share_in,
    send_sem,
    recv_sem,
    kept_sem,
    log_send,
    log_recv,
    out_send,
    out_recv,
    sq_send,
    sq_recv,
    share_send,
    share_recv,
):
    ctx, head = peers
    me = lax.axis_index("ctx")
    plane = lax.axis_index("head")
    blocks = log_ref.shape[1]
    total_blocks = ctx * blocks
    others = ORDER

    barrier = pltpu.get_barrier_semaphore()
    for bits in others:
        pl.semaphore_signal(
            barrier, inc=1, device_id=(flipped(me, bits), plane), device_id_type=MESH
        )
    for step in range(1, head):
        pl.semaphore_signal(
            barrier, inc=1, device_id=(me, (plane + step) % head), device_id_type=MESH
        )
    pl.semaphore_wait(barrier, ctx - 1 + head - 1)

    pairs = ((k_hbm, k_all), (v_hbm, v_all), (q_hbm, q_all))
    stages = stage_list(blocks)

    def columns(index):
        return pl.ds(pl.multiple_of(index * BLOCK, BLOCK), BLOCK)

    def span(index, low=0, count=blocks):
        return pl.ds(index * blocks + low, count)

    def remote(source, target, send, recv, there):
        return pltpu.make_async_remote_copy(
            src_ref=source,
            dst_ref=target,
            send_sem=send,
            recv_sem=recv,
            device_id=(there, plane),
            device_id_type=MESH,
        )

    def row_copies(stage, bits, arriving):
        arrays, low, count, slot = stages[stage]
        there = flipped(me, bits)
        origin = there if arriving else me
        return [
            remote(
                pairs[which][0].at[pl.ds(low, count), :, columns(there)],
                pairs[which][1].at[span(origin, low, count)],
                send_sem.at[slot + extra, bits],
                recv_sem.at[slot + extra, bits],
                there,
            )
            for extra, which in enumerate(arrays)
        ]

    def log_copy(bits, arriving):
        there = flipped(me, bits)
        origin = there if arriving else me
        return remote(
            log_ref.at[there], log_all.at[origin], log_send.at[bits], log_recv.at[bits], there
        )

    sequence = [turned(me, bits) for bits in others]

    def begin(stage):
        for bits in sequence:
            for copy in row_copies(stage, bits, False):
                copy.start()

    def sent(stage):
        for bits in others:
            for copy in row_copies(stage, bits, False):
                copy.wait_send()

    def arrived(stage):
        for bits in others:
            for copy in row_copies(stage, bits, True):
                copy.wait_recv()

    for bits in others:
        log_copy(bits, False).start()
    for stage in range(AHEAD):
        begin(stage)
    kept = [
        pltpu.make_async_copy(
            source.at[:, :, columns(me)], landing.at[span(me)], kept_sem.at[index]
        )
        for index, (source, landing) in enumerate(pairs)
    ]
    kept.append(pltpu.make_async_copy(log_ref.at[me], log_all.at[me], kept_sem.at[ARRAYS]))
    for copy in kept:
        copy.start()

    sub = lax.broadcasted_iota(jnp.int32, (BLOCK, BLOCK), 0)
    lane = lax.broadcasted_iota(jnp.int32, (BLOCK, BLOCK), 1)
    along = lax.broadcasted_iota(jnp.int32, (1, BLOCK), 1)

    starts = [jnp.int32(0)]
    for index in range(length_ref.shape[0] - 1):
        starts.append(starts[-1] + length_ref[index])

    def mark(block, carry):
        base = packing_ref[block] * BLOCK
        begins = jnp.full((1, BLOCK), -(1 << 24), jnp.int32)
        broken_at = jnp.full((1, BLOCK), BLOCK, jnp.int32)
        for start in starts:
            relative = jnp.broadcast_to(start - base, (1, BLOCK))
            begins = jnp.maximum(begins, jnp.where(relative <= along, relative, -(1 << 24)))
            broken_at = jnp.minimum(broken_at, jnp.where(relative >= 0, relative, BLOCK))
        meta[block, 0:1, :] = begins
        meta[block, 1:2, :] = broken_at
        meta[block, 2:3, :] = jnp.broadcast_to(begins[:, BLOCK - 1 :], (1, BLOCK))
        return carry

    lax.fori_loop(0, total_blocks, mark, 0)
    for copy in kept:
        copy.wait()
    for bits in others:
        log_copy(bits, True).wait_recv()

    def down(row):
        return jnp.transpose(jnp.broadcast_to(row, (BLOCK, BLOCK)))

    def key_block(there, index):
        block = there * blocks + index
        log_row = log_all[there, index : index + 1, :]
        last_begin = meta[block, 2:3, :]
        total = jnp.broadcast_to(log_row[:, BLOCK - 1 :], (1, BLOCK))
        keep = jnp.where(along >= last_begin, jnp.exp(total - log_row), 0.0)
        decayed = (k_all[block].astype(jnp.float32) * down(keep)).astype(jnp.bfloat16)
        own[block] = contract(decayed, v_all[block], 0, 0)
        gate[block] = jnp.where(last_begin < 0, jnp.exp(total), 0.0)

    def query_block(there, index):
        block = there * blocks + index
        log_row = log_all[there, index : index + 1, :]
        begins = meta[block, 0:1, :]
        broken_at = meta[block, 1:2, :]
        queries = q_all[block]
        scores = contract(k_all[block], queries, 1, 1)
        allowed = (sub >= begins) & (sub <= lane)
        gaps = jnp.minimum(log_row - down(log_row), 0.0)
        weights = jnp.where(allowed, scores * jnp.exp(gaps), 0.0).astype(jnp.bfloat16)
        intra[block] = contract(weights, v_all[block], 0, 0)
        reach = jnp.where(along < broken_at, jnp.exp(log_row), 0.0)
        q_all[block] = (queries.astype(jnp.float32) * down(reach)).astype(jnp.bfloat16)

    def work(stage):
        arrays, low, count, slot = stages[stage]
        each = key_block if len(arrays) > 1 else query_block
        at_once = max(1, 4 // count)

        def several(step, carry):
            for extra in range(at_once):
                for index in range(low, low + count):
                    each(step * at_once + extra, index)
            return carry

        lax.fori_loop(0, ctx // at_once, several, 0)

    def advance(step, state):
        for extra in range(4):
            place = step * 4 + extra
            block = source_ref[place]
            states[place] = state.astype(jnp.bfloat16)
            state = gate[block] * state + own[block]
        return state

    for stage in range(len(stages)):
        arrived(stage)
        if stage + AHEAD < len(stages):
            sent(stage)
            begin(stage + AHEAD)
        work(stage)
        if stage + 1 < len(stages) and len(stages[stage][0]) > len(stages[stage + 1][0]):
            zero_state = jnp.zeros((BLOCK, BLOCK), jnp.float32)
            lax.fori_loop(0, total_blocks // 4, advance, zero_state)

    ones = jnp.ones((8, BLOCK), jnp.bfloat16)

    def out_copy(bits, arriving):
        there = flipped(me, bits)
        origin = there if arriving else me
        return remote(
            out_all.at[span(there)],
            out_hbm.at[:, :, columns(origin)],
            out_send.at[bits],
            out_recv.at[bits],
            there,
        )

    def sq_copy(bits, arriving):
        there = flipped(me, bits)
        origin = there if arriving else me
        return remote(
            squares.at[there], squares_in.at[origin], sq_send.at[bits], sq_recv.at[bits], there
        )

    def finish(there):
        def several(step, carry):
            for extra in range(4):
                index = step * 4 + extra
                place = there * blocks + index
                block = source_ref[place]
                result = intra[block] + contract(q_all[block], states[place], 1, 0)
                out_all[place] = result.astype(jnp.bfloat16)
                summed = contract(ones, (result * result).astype(jnp.bfloat16), 1, 1)
                squares[there, pl.ds(index, 1), :] = summed[0:1]
            return carry

        lax.fori_loop(0, blocks // 4, several, 0)

    for index, bits in enumerate(sequence):
        finish(flipped(me, bits))
        if index < 4:
            out_copy(bits, False).start()
    for bits in others:
        sq_copy(bits, False).start()
    for bits in sequence[4:]:
        out_copy(bits, False).start()
    finish(me)
    kept_out = pltpu.make_async_copy(
        out_all.at[span(me)], out_hbm.at[:, :, columns(me)], kept_sem.at[0]
    )
    kept_out.start()
    summed = squares[me]
    for bits in others:
        sq_copy(bits, True).wait_recv()
        summed = summed + squares_in[flipped(me, bits)]
    share_in[plane] = summed

    def share_copy(step, slot):
        return pltpu.make_async_remote_copy(
            src_ref=share_in.at[plane],
            dst_ref=share_in.at[slot],
            send_sem=share_send.at[step],
            recv_sem=share_recv.at[step],
            device_id=(me, (plane + step) % head),
            device_id_type=MESH,
        )

    for step in range(1, head):
        share_copy(step, plane).start()
    total = summed
    for step in range(1, head):
        origin = (plane + head - step) % head
        share_copy(step, origin).wait_recv()
        total = total + share_in[origin]
    total_ref[...] = total
    for stage in range(len(stages) - AHEAD, len(stages)):
        sent(stage)
    kept_out.wait()
    for bits in others:
        out_copy(bits, True).wait_recv()
    for bits in others:
        log_copy(bits, False).wait_send()
        out_copy(bits, False).wait_send()
        sq_copy(bits, False).wait_send()
    for step in range(1, head):
        share_copy(step, plane).wait_send()


def by_head(queries, key_rows, value_rows, log_decay, norm_gain, doc_lengths, packing):
    rows, width = queries.shape
    heads = log_decay.shape[1]
    blocks = rows // BLOCK
    ctx = lax.axis_size("ctx")
    head = lax.axis_size("head")
    total_blocks = packing.shape[0]

    order = jnp.arange(BLOCK)
    lower = (order[:, None] >= order[None, :]).astype(jnp.bfloat16)
    logs = jnp.einsum(
        "ts,nsh->hnt",
        lower,
        log_decay.reshape(blocks, BLOCK, heads),
        preferred_element_type=jnp.float32,
    )
    places = jnp.arange(total_blocks, dtype=jnp.int32)
    source = jnp.sum(
        jnp.where(packing[None, :] == places[:, None], places[None, :], 0), axis=1
    ).astype(jnp.int32)

    def in_blocks(values):
        return values.reshape(blocks, BLOCK, width)

    copies = sum(len(stage[0]) for stage in stage_list(blocks))
    any_spec = pl.BlockSpec(memory_space=pl.ANY)
    vmem = pl.BlockSpec(memory_space=pltpu.VMEM)
    dma = pltpu.SemaphoreType.DMA
    out, squares = pl.pallas_call(
        functools.partial(attention_kernel, (ctx, head)),
        out_shape=(
            jax.ShapeDtypeStruct((blocks, BLOCK, width), jnp.bfloat16),
            jax.ShapeDtypeStruct((blocks, BLOCK), jnp.float32),
        ),
        in_specs=[any_spec] * 3 + [vmem] + [pl.BlockSpec(memory_space=pltpu.SMEM)] * 3,
        out_specs=(any_spec, vmem),
        scratch_shapes=[
            pltpu.VMEM((total_blocks, BLOCK, BLOCK), jnp.bfloat16),
            pltpu.VMEM((total_blocks, BLOCK, BLOCK), jnp.bfloat16),
            pltpu.VMEM((total_blocks, BLOCK, BLOCK), jnp.bfloat16),
            pltpu.VMEM((ctx, blocks, BLOCK), jnp.float32),
            pltpu.VMEM((total_blocks, 8, BLOCK), jnp.int32),
            pltpu.VMEM((total_blocks, BLOCK, BLOCK), jnp.float32),
            pltpu.VMEM((total_blocks, BLOCK, BLOCK), jnp.float32),
            pltpu.VMEM((total_blocks, 1, BLOCK), jnp.float32),
            pltpu.VMEM((total_blocks, BLOCK, BLOCK), jnp.bfloat16),
            pltpu.VMEM((total_blocks, BLOCK, BLOCK), jnp.bfloat16),
            pltpu.VMEM((ctx, blocks, BLOCK), jnp.float32),
            pltpu.VMEM((ctx, blocks, BLOCK), jnp.float32),
            pltpu.VMEM((head, blocks, BLOCK), jnp.float32),
            dma((copies, ctx)),
            dma((copies, ctx)),
            dma((ARRAYS + 1,)),
            dma((ctx,)),
            dma((ctx,)),
            dma((ctx,)),
            dma((ctx,)),
            dma((ctx,)),
            dma((ctx,)),
            dma((head,)),
            dma((head,)),
        ],
        compiler_params=pltpu.CompilerParams(
            collective_id=0, has_side_effects=True, vmem_limit_bytes=52 * 1024 * 1024
        ),
        name="attention_by_head",
    )(in_blocks(queries), in_blocks(key_rows), in_blocks(value_rows), logs, doc_lengths, packing, source)
    scale = lax.rsqrt(squares / (width * head) + 1e-05)
    normed = out.astype(jnp.float32) * scale[:, :, None] * norm_gain[None, None, :]
    return normed.astype(jnp.bfloat16).reshape(rows, width)


def from_behind(x, axis, by):
    count = lax.axis_size(axis)
    pairs = [(i, i + by) for i in range(count) if 0 <= i + by < count]
    return lax.ppermute(x, axis, pairs)


def state_pass(key_blocks, value_blocks, decay_blocks, first, docid):
    block_log = jnp.cumsum(decay_blocks.astype(jnp.float32), axis=1)
    block_total = block_log[:, -1, :]
    seen = jnp.cumsum(first, axis=1)
    reach_block = (seen == 0).astype(jnp.float32)
    unbroken = (seen[:, -1] == 0).astype(jnp.float32)
    same_last = (docid == docid[:, -1:]).astype(jnp.float32)
    keep = jnp.exp(block_total[:, None, :] - block_log) * same_last[:, :, None]
    key_decayed = (key_blocks.astype(jnp.float32) * keep[..., None]).astype(jnp.bfloat16)
    own = jnp.einsum(
        "nshd,nshe->nhde", key_decayed, value_blocks, preferred_element_type=jnp.float32
    )
    gate = jnp.exp(block_total) * unbroken[:, None]

    def advance(state, item):
        factor, term = item
        return (factor[:, None, None] * state + term, state)

    start = jnp.zeros(own.shape[1:], jnp.float32)
    s_end, states = lax.scan(advance, start, (gate, own))
    prior = jnp.cumsum(block_total, axis=0) - block_total
    segment_log = block_log + prior[:, None, :]
    block_starts = seen[:, -1]
    before = jnp.cumsum(block_starts) - block_starts
    reach_segment = (seen + before[:, None] == 0).astype(jnp.float32)
    clean = (jnp.sum(first) == 0).astype(jnp.float32)
    decay_all = jnp.exp(segment_log[-1, -1]) * clean
    return (block_log, reach_block, states, segment_log, reach_segment, decay_all, s_end)


def query_pass(query_blocks, key_blocks, value_blocks, block_log, reach_block, states, docid):
    length = docid.shape[1]
    order = jnp.arange(length)
    causal = order[:, None] >= order[None, :]
    allowed = causal[None] & (docid[:, :, None] == docid[:, None, :])
    by_head = jnp.transpose(block_log, (0, 2, 1))
    gaps = by_head[:, :, :, None] - by_head[:, :, None, :]
    weight = jnp.where(allowed[:, None], jnp.exp(jnp.minimum(gaps, 0.0)), 0.0)
    scores = jnp.einsum(
        "nthd,nshd->nhts", query_blocks, key_blocks, preferred_element_type=jnp.float32
    )
    weights = (scores * weight).astype(jnp.bfloat16)
    intra = jnp.einsum("nhts,nshd->nthd", weights, value_blocks, preferred_element_type=jnp.float32)
    query_decayed = (
        query_blocks.astype(jnp.float32) * (jnp.exp(block_log) * reach_block[:, :, None])[..., None]
    ).astype(jnp.bfloat16)
    inter = jnp.einsum(
        "nthd,nhde->nthe",
        query_decayed,
        states.astype(jnp.bfloat16),
        preferred_element_type=jnp.float32,
    )
    return intra + inter


def carry_in(decay_all, s_end, devices):
    zero_state = jnp.zeros(s_end.shape, jnp.float32)

    def forward(index, pair):
        arrived = from_behind(pair[1], "ctx", 1)
        return (arrived, decay_all[:, None, None] * arrived + s_end)

    arrival, leaving = lax.fori_loop(0, devices - 1, forward, (zero_state, s_end))
    return arrival


def body(queries, key_rows, value_rows, log_decay, norm_gain, doc_lengths, packing):
    rows, width = queries.shape
    heads = log_decay.shape[1]
    head_size = width // heads
    blocks = rows // BLOCK
    devices = lax.axis_size("ctx")
    mine = lax.axis_index("ctx")
    total_blocks = packing.shape[0]
    capacity = (2 * blocks + devices - 1) // devices
    owners = (packing // blocks).reshape(devices, blocks)
    local = jnp.arange(blocks, dtype=jnp.int32)
    earlier_mask = local[:, None] < local[None, :]
    same_owner = owners[:, :, None] == owners[:, None, :]
    ranks = jnp.sum((same_owner & earlier_mask[None]).astype(jnp.int32), axis=1)
    my_owner = lax.dynamic_index_in_dim(owners, mine, 0, keepdims=False)
    my_rank = lax.dynamic_index_in_dim(ranks, mine, 0, keepdims=False)
    slot_of = my_owner * capacity + my_rank
    slot_ids = jnp.arange(devices * capacity, dtype=jnp.int32)
    matched = slot_of[None, :] == slot_ids[:, None]
    source = jnp.sum(matched.astype(jnp.int32) * local[None, :], axis=1)
    filled = jnp.any(matched, axis=1)

    def outgoing(values):
        columns = values.shape[1]
        picked = jnp.take(values.reshape(blocks, BLOCK, columns), source, axis=0)
        kept = jnp.where(filled[:, None, None], picked, jnp.zeros((), values.dtype))
        return kept.reshape(devices, capacity * BLOCK, columns)

    target = mine * blocks + local
    block_index = jnp.arange(total_blocks, dtype=jnp.int32)
    wanted = packing[None, :] == target[:, None]
    loader_block = jnp.sum(wanted.astype(jnp.int32) * block_index[None, :], axis=1)
    column = loader_block // blocks * capacity + jnp.take(ranks.reshape(-1), loader_block)

    def arriving(values):
        return jnp.take(values.reshape(devices * capacity, BLOCK, values.shape[2]), column, axis=0)

    starts = jnp.cumsum(doc_lengths) - doc_lengths
    positions = mine * rows + jnp.arange(rows, dtype=jnp.int32)
    first = (
        jnp.any(positions[:, None] == starts[None, :], axis=1)
        .astype(jnp.int32)
        .reshape(blocks, BLOCK)
    )
    docid = (
        jnp.sum((starts[None, :] <= positions[:, None]).astype(jnp.int32), axis=1) - 1
    ).reshape(blocks, BLOCK)
    got_queries, got_keys, got_values, received_decay = (
        lax.all_to_all(outgoing(queries), "ctx", split_axis=0, concat_axis=0, tiled=True),
        lax.all_to_all(outgoing(key_rows), "ctx", split_axis=0, concat_axis=0, tiled=True),
        lax.all_to_all(outgoing(value_rows), "ctx", split_axis=0, concat_axis=0, tiled=True),
        lax.all_to_all(outgoing(log_decay), "ctx", split_axis=0, concat_axis=0, tiled=True),
    )
    key_blocks = arriving(got_keys).reshape(blocks, BLOCK, heads, head_size)
    value_blocks = arriving(got_values).reshape(blocks, BLOCK, heads, head_size)
    decay_blocks = arriving(received_decay)
    block_log, reach_block, states, segment_log, reach_segment, decay_all, s_end = state_pass(
        key_blocks, value_blocks, decay_blocks, first, docid
    )
    arrival = carry_in(decay_all, s_end, devices)
    query_blocks = arriving(got_queries).reshape(blocks, BLOCK, heads, head_size)
    local_out = query_pass(
        query_blocks, key_blocks, value_blocks, block_log, reach_block, states, docid
    )
    scaled = (
        query_blocks.astype(jnp.float32)
        * (jnp.exp(segment_log) * reach_segment[:, :, None])[..., None]
    ).astype(jnp.bfloat16)
    carried = jnp.einsum(
        "nthd,hde->nthe", scaled, arrival.astype(jnp.bfloat16), preferred_element_type=jnp.float32
    )
    total = (local_out + carried).reshape(rows, width)
    squares = lax.psum(jnp.sum(total * total, axis=1), "head")
    columns_all = width * lax.axis_size("head")
    scale = lax.rsqrt(squares / columns_all + 1e-05)
    return (total * scale[:, None] * norm_gain[None, :]).astype(jnp.bfloat16)


def solution(mesh):
    placed = (
        P("ctx", "head"),
        P("ctx", "head"),
        P("ctx", "head"),
        P("ctx", "head"),
        P("head"),
        P(),
        P(),
    )
    one_head_each = mesh.shape["ctx"] == 8 and mesh.shape["head"] == 4
    return jax.shard_map(
        by_head if one_head_each else body, mesh=mesh, in_specs=placed, out_specs=P("ctx", "head"), check_vma=False
    )
```

```python
import functools

import jax
import jax.numpy as jnp
from jax import lax
from jax.experimental import pallas as pl
from jax.experimental.pallas import tpu as pltpu
from jax.sharding import PartitionSpec as P

BLOCK = 128
MESH = pl.DeviceIdType.MESH
ORDER = (4, 2, 5, 3, 6, 7, 1)
ARRAYS = 3
AHEAD = 2


def stage_list(blocks):
    stages = []
    slot = 0
    for low in range(0, blocks, 4):
        stages.append(((0, 1), low, 4, slot))
        slot += 2
    for low in range(0, blocks, 2):
        stages.append(((2,), low, 2, slot))
        slot += 1
    return stages


def flipped(me, bits):
    high, mid, low = me // 4, (me // 2) % 2, me % 2
    return (
        4 * ((high + bits // 4) % 2) + 2 * ((mid + bits // 2 % 2) % 2) + (low + bits % 2) % 2
    )


def turned(me, bits):
    swapped = 4 * (bits // 2 % 2) + 2 * (bits // 4) + bits % 2
    return bits + (swapped - bits) * (me % 2)


def contract(a, b, dim_a, dim_b):
    return lax.dot_general(
        a, b, (((dim_a,), (dim_b,)), ((), ())), preferred_element_type=jnp.float32
    )


def attention_kernel(
    peers,
    q_hbm,
    k_hbm,
    v_hbm,
    log_ref,
    length_ref,
    packing_ref,
    source_ref,
    out_hbm,
    total_ref,
    q_all,
    k_all,
    v_all,
    log_all,
    meta,
    intra,
    own,
    gate,
    states,
    out_all,
    squares,
    squares_in,
    share_in,
    k_held,
    v_held,
    q_held,
    held_sem,
    send_sem,
    recv_sem,
    kept_sem,
    log_send,
    log_recv,
    out_send,
    out_recv,
    sq_send,
    sq_recv,
    share_send,
    share_recv,
):
    ctx, head = peers
    me = lax.axis_index("ctx")
    plane = lax.axis_index("head")
    blocks = log_ref.shape[1]
    total_blocks = ctx * blocks
    others = ORDER

    def columns(index):
        return pl.ds(pl.multiple_of(index * BLOCK, BLOCK), BLOCK)

    held = ((k_hbm, k_held), (v_hbm, v_held), (q_hbm, q_held))

    def hold(which, bits):
        there = flipped(me, bits)
        return pltpu.make_async_copy(
            held[which][0].at[:, :, columns(there)],
            held[which][1].at[pl.ds(there * blocks, blocks)],
            held_sem.at[which, bits],
        )

    for which in range(ARRAYS):
        for bits in others:
            hold(which, bits).start()

    barrier = pltpu.get_barrier_semaphore()
    for bits in others:
        pl.semaphore_signal(
            barrier, inc=1, device_id=(flipped(me, bits), plane), device_id_type=MESH
        )
    for step in range(1, head):
        pl.semaphore_signal(
            barrier, inc=1, device_id=(me, (plane + step) % head), device_id_type=MESH
        )
    pl.semaphore_wait(barrier, ctx - 1 + head - 1)

    pairs = ((k_hbm, k_all), (v_hbm, v_all), (q_hbm, q_all))
    stages = stage_list(blocks)

    def span(index, low=0, count=blocks):
        return pl.ds(index * blocks + low, count)

    def remote(source, target, send, recv, there):
        return pltpu.make_async_remote_copy(
            src_ref=source,
            dst_ref=target,
            send_sem=send,
            recv_sem=recv,
            device_id=(there, plane),
            device_id_type=MESH,
        )

    def row_copies(stage, bits, arriving):
        arrays, low, count, slot = stages[stage]
        there = flipped(me, bits)
        origin = there if arriving else me
        return [
            remote(
                held[which][1].at[span(there, low, count)],
                pairs[which][1].at[span(origin, low, count)],
                send_sem.at[slot + extra, bits],
                recv_sem.at[slot + extra, bits],
                there,
            )
            for extra, which in enumerate(arrays)
        ]

    def log_copy(bits, arriving):
        there = flipped(me, bits)
        origin = there if arriving else me
        return remote(
            log_ref.at[there], log_all.at[origin], log_send.at[bits], log_recv.at[bits], there
        )

    sequence = [turned(me, bits) for bits in others]

    def begin(stage):
        for bits in sequence:
            for copy in row_copies(stage, bits, False):
                copy.start()

    def sent(stage):
        for bits in others:
            for copy in row_copies(stage, bits, False):
                copy.wait_send()

    def arrived(stage):
        for bits in others:
            for copy in row_copies(stage, bits, True):
                copy.wait_recv()

    for bits in others:
        log_copy(bits, False).start()
    for which in range(2):
        for bits in others:
            hold(which, bits).wait()
    for stage in range(AHEAD):
        begin(stage)
    for bits in others:
        hold(2, bits).wait()
    kept = [
        pltpu.make_async_copy(
            source.at[:, :, columns(me)], landing.at[span(me)], kept_sem.at[index]
        )
        for index, (source, landing) in enumerate(pairs)
    ]
    kept.append(pltpu.make_async_copy(log_ref.at[me], log_all.at[me], kept_sem.at[ARRAYS]))
    for copy in kept:
        copy.start()

    sub = lax.broadcasted_iota(jnp.int32, (BLOCK, BLOCK), 0)
    lane = lax.broadcasted_iota(jnp.int32, (BLOCK, BLOCK), 1)
    along = lax.broadcasted_iota(jnp.int32, (1, BLOCK), 1)

    starts = [jnp.int32(0)]
    for index in range(length_ref.shape[0] - 1):
        starts.append(starts[-1] + length_ref[index])

    def mark(block, carry):
        base = packing_ref[block] * BLOCK
        begins = jnp.full((1, BLOCK), -(1 << 24), jnp.int32)
        broken_at = jnp.full((1, BLOCK), BLOCK, jnp.int32)
        for start in starts:
            relative = jnp.broadcast_to(start - base, (1, BLOCK))
            begins = jnp.maximum(begins, jnp.where(relative <= along, relative, -(1 << 24)))
            broken_at = jnp.minimum(broken_at, jnp.where(relative >= 0, relative, BLOCK))
        meta[block, 0:1, :] = begins
        meta[block, 1:2, :] = broken_at
        meta[block, 2:3, :] = jnp.broadcast_to(begins[:, BLOCK - 1 :], (1, BLOCK))
        return carry

    lax.fori_loop(0, total_blocks, mark, 0)
    for copy in kept:
        copy.wait()
    for bits in others:
        log_copy(bits, True).wait_recv()

    def down(row):
        return jnp.transpose(jnp.broadcast_to(row, (BLOCK, BLOCK)))

    def key_block(there, index):
        block = there * blocks + index
        log_row = log_all[there, index : index + 1, :]
        last_begin = meta[block, 2:3, :]
        total = jnp.broadcast_to(log_row[:, BLOCK - 1 :], (1, BLOCK))
        keep = jnp.where(along >= last_begin, jnp.exp(total - log_row), 0.0)
        decayed = (k_all[block].astype(jnp.float32) * down(keep)).astype(jnp.bfloat16)
        own[block] = contract(decayed, v_all[block], 0, 0)
        gate[block] = jnp.where(last_begin < 0, jnp.exp(total), 0.0)

    def query_block(there, index):
        block = there * blocks + index
        log_row = log_all[there, index : index + 1, :]
        begins = meta[block, 0:1, :]
        broken_at = meta[block, 1:2, :]
        queries = q_all[block]
        scores = contract(k_all[block], queries, 1, 1)
        allowed = (sub >= begins) & (sub <= lane)
        gaps = jnp.minimum(log_row - down(log_row), 0.0)
        weights = jnp.where(allowed, scores * jnp.exp(gaps), 0.0).astype(jnp.bfloat16)
        intra[block] = contract(weights, v_all[block], 0, 0)
        reach = jnp.where(along < broken_at, jnp.exp(log_row), 0.0)
        q_all[block] = (queries.astype(jnp.float32) * down(reach)).astype(jnp.bfloat16)

    def work(stage):
        arrays, low, count, slot = stages[stage]
        each = key_block if len(arrays) > 1 else query_block
        at_once = max(1, 4 // count)

        def several(step, carry):
            for extra in range(at_once):
                for index in range(low, low + count):
                    each(step * at_once + extra, index)
            return carry

        lax.fori_loop(0, ctx // at_once, several, 0)

    def advance(step, state):
        for extra in range(4):
            place = step * 4 + extra
            block = source_ref[place]
            states[place] = state.astype(jnp.bfloat16)
            state = gate[block] * state + own[block]
        return state

    for stage in range(len(stages)):
        arrived(stage)
        if stage + AHEAD < len(stages):
            sent(stage)
            begin(stage + AHEAD)
        work(stage)
        if stage + 1 < len(stages) and len(stages[stage][0]) > len(stages[stage + 1][0]):
            zero_state = jnp.zeros((BLOCK, BLOCK), jnp.float32)
            lax.fori_loop(0, total_blocks // 4, advance, zero_state)

    ones = jnp.ones((8, BLOCK), jnp.bfloat16)

    def out_copy(bits, arriving):
        there = flipped(me, bits)
        origin = there if arriving else me
        return remote(
            out_all.at[span(there)],
            out_hbm.at[origin],
            out_send.at[bits],
            out_recv.at[bits],
            there,
        )

    def sq_copy(bits, arriving):
        there = flipped(me, bits)
        origin = there if arriving else me
        return remote(
            squares.at[there], squares_in.at[origin], sq_send.at[bits], sq_recv.at[bits], there
        )

    def finish(there):
        def several(step, carry):
            for extra in range(4):
                index = step * 4 + extra
                place = there * blocks + index
                block = source_ref[place]
                result = intra[block] + contract(q_all[block], states[place], 1, 0)
                out_all[place] = result.astype(jnp.bfloat16)
                summed = contract(ones, (result * result).astype(jnp.bfloat16), 1, 1)
                squares[there, pl.ds(index, 1), :] = summed[0:1]
            return carry

        lax.fori_loop(0, blocks // 4, several, 0)

    for index, bits in enumerate(sequence):
        finish(flipped(me, bits))
        if index < 4:
            out_copy(bits, False).start()
    for bits in others:
        sq_copy(bits, False).start()
    for bits in sequence[4:]:
        out_copy(bits, False).start()
    finish(me)
    kept_out = pltpu.make_async_copy(
        out_all.at[span(me)], out_hbm.at[me], kept_sem.at[0]
    )
    kept_out.start()
    summed = squares[me]
    for bits in others:
        sq_copy(bits, True).wait_recv()
        summed = summed + squares_in[flipped(me, bits)]
    share_in[plane] = summed

    def share_copy(step, slot):
        return pltpu.make_async_remote_copy(
            src_ref=share_in.at[plane],
            dst_ref=share_in.at[slot],
            send_sem=share_send.at[step],
            recv_sem=share_recv.at[step],
            device_id=(me, (plane + step) % head),
            device_id_type=MESH,
        )

    for step in range(1, head):
        share_copy(step, plane).start()
    total = summed
    for step in range(1, head):
        origin = (plane + head - step) % head
        share_copy(step, origin).wait_recv()
        total = total + share_in[origin]
    total_ref[...] = total
    for stage in range(len(stages) - AHEAD, len(stages)):
        sent(stage)
    kept_out.wait()
    for bits in others:
        out_copy(bits, True).wait_recv()
    for bits in others:
        log_copy(bits, False).wait_send()
        out_copy(bits, False).wait_send()
        sq_copy(bits, False).wait_send()
    for step in range(1, head):
        share_copy(step, plane).wait_send()


def norm_kernel(count, out_ref, squares_ref, gain_ref, mixed_ref):
    scale = lax.rsqrt(squares_ref[0] / count + 1e-05)
    down = jnp.transpose(jnp.broadcast_to(scale, (BLOCK, BLOCK)))
    for index in range(out_ref.shape[0]):
        at = slice(index * BLOCK, (index + 1) * BLOCK)
        values = out_ref[index, 0].astype(jnp.float32) * down * gain_ref[:, at]
        mixed_ref[:, at] = values.astype(jnp.bfloat16)


def by_head(queries, key_rows, value_rows, log_decay, norm_gain, doc_lengths, packing):
    rows, width = queries.shape
    heads = log_decay.shape[1]
    blocks = rows // BLOCK
    ctx = lax.axis_size("ctx")
    head = lax.axis_size("head")
    total_blocks = packing.shape[0]

    order = jnp.arange(BLOCK)
    lower = (order[:, None] >= order[None, :]).astype(jnp.bfloat16)
    logs = jnp.einsum(
        "ts,nsh->hnt",
        lower,
        log_decay.reshape(blocks, BLOCK, heads),
        preferred_element_type=jnp.float32,
    )
    places = jnp.arange(total_blocks, dtype=jnp.int32)
    source = jnp.sum(
        jnp.where(packing[None, :] == places[:, None], places[None, :], 0), axis=1
    ).astype(jnp.int32)

    def in_blocks(values):
        return values.reshape(blocks, BLOCK, width)

    copies = sum(len(stage[0]) for stage in stage_list(blocks))
    any_spec = pl.BlockSpec(memory_space=pl.ANY)
    vmem = pl.BlockSpec(memory_space=pltpu.VMEM)
    dma = pltpu.SemaphoreType.DMA
    out, squares = pl.pallas_call(
        functools.partial(attention_kernel, (ctx, head)),
        out_shape=(
            jax.ShapeDtypeStruct((ctx, blocks, BLOCK, BLOCK), jnp.bfloat16),
            jax.ShapeDtypeStruct((blocks, BLOCK), jnp.float32),
        ),
        in_specs=[any_spec] * 3 + [vmem] + [pl.BlockSpec(memory_space=pltpu.SMEM)] * 3,
        out_specs=(any_spec, vmem),
        scratch_shapes=[
            pltpu.VMEM((total_blocks, BLOCK, BLOCK), jnp.bfloat16),
            pltpu.VMEM((total_blocks, BLOCK, BLOCK), jnp.bfloat16),
            pltpu.VMEM((total_blocks, BLOCK, BLOCK), jnp.bfloat16),
            pltpu.VMEM((ctx, blocks, BLOCK), jnp.float32),
            pltpu.VMEM((total_blocks, 8, BLOCK), jnp.int32),
            pltpu.VMEM((total_blocks, BLOCK, BLOCK), jnp.float32),
            pltpu.VMEM((total_blocks, BLOCK, BLOCK), jnp.float32),
            pltpu.VMEM((total_blocks, 1, BLOCK), jnp.float32),
            pltpu.VMEM((total_blocks, BLOCK, BLOCK), jnp.bfloat16),
            pltpu.VMEM((total_blocks, BLOCK, BLOCK), jnp.bfloat16),
            pltpu.VMEM((ctx, blocks, BLOCK), jnp.float32),
            pltpu.VMEM((ctx, blocks, BLOCK), jnp.float32),
            pltpu.VMEM((head, blocks, BLOCK), jnp.float32),
            pltpu.VMEM((total_blocks, BLOCK, BLOCK), jnp.bfloat16),
            pltpu.VMEM((total_blocks, BLOCK, BLOCK), jnp.bfloat16),
            pltpu.VMEM((total_blocks, BLOCK, BLOCK), jnp.bfloat16),
            dma((ARRAYS, ctx)),
            dma((copies, ctx)),
            dma((copies, ctx)),
            dma((ARRAYS + 1,)),
            dma((ctx,)),
            dma((ctx,)),
            dma((ctx,)),
            dma((ctx,)),
            dma((ctx,)),
            dma((ctx,)),
            dma((head,)),
            dma((head,)),
        ],
        compiler_params=pltpu.CompilerParams(
            collective_id=0, has_side_effects=True, vmem_limit_bytes=58 * 1024 * 1024
        ),
        name="attention_by_head",
    )(in_blocks(queries), in_blocks(key_rows), in_blocks(value_rows), logs, doc_lengths, packing, source)
    return pl.pallas_call(
        functools.partial(norm_kernel, width * head),
        grid=(blocks,),
        out_shape=jax.ShapeDtypeStruct((rows, width), jnp.bfloat16),
        in_specs=[
            pl.BlockSpec((ctx, 1, BLOCK, BLOCK), lambda n: (0, n, 0, 0)),
            pl.BlockSpec((1, 1, BLOCK), lambda n: (n, 0, 0)),
            pl.BlockSpec((1, width), lambda n: (0, 0)),
        ],
        out_specs=pl.BlockSpec((BLOCK, width), lambda n: (n, 0)),
        name="norm_rows",
    )(out, squares.reshape(blocks, 1, BLOCK), norm_gain.reshape(1, width))


def from_behind(x, axis, by):
    count = lax.axis_size(axis)
    pairs = [(i, i + by) for i in range(count) if 0 <= i + by < count]
    return lax.ppermute(x, axis, pairs)


def state_pass(key_blocks, value_blocks, decay_blocks, first, docid):
    block_log = jnp.cumsum(decay_blocks.astype(jnp.float32), axis=1)
    block_total = block_log[:, -1, :]
    seen = jnp.cumsum(first, axis=1)
    reach_block = (seen == 0).astype(jnp.float32)
    unbroken = (seen[:, -1] == 0).astype(jnp.float32)
    same_last = (docid == docid[:, -1:]).astype(jnp.float32)
    keep = jnp.exp(block_total[:, None, :] - block_log) * same_last[:, :, None]
    key_decayed = (key_blocks.astype(jnp.float32) * keep[..., None]).astype(jnp.bfloat16)
    own = jnp.einsum(
        "nshd,nshe->nhde", key_decayed, value_blocks, preferred_element_type=jnp.float32
    )
    gate = jnp.exp(block_total) * unbroken[:, None]

    def advance(state, item):
        factor, term = item
        return (factor[:, None, None] * state + term, state)

    start = jnp.zeros(own.shape[1:], jnp.float32)
    s_end, states = lax.scan(advance, start, (gate, own))
    prior = jnp.cumsum(block_total, axis=0) - block_total
    segment_log = block_log + prior[:, None, :]
    block_starts = seen[:, -1]
    before = jnp.cumsum(block_starts) - block_starts
    reach_segment = (seen + before[:, None] == 0).astype(jnp.float32)
    clean = (jnp.sum(first) == 0).astype(jnp.float32)
    decay_all = jnp.exp(segment_log[-1, -1]) * clean
    return (block_log, reach_block, states, segment_log, reach_segment, decay_all, s_end)


def query_pass(query_blocks, key_blocks, value_blocks, block_log, reach_block, states, docid):
    length = docid.shape[1]
    order = jnp.arange(length)
    causal = order[:, None] >= order[None, :]
    allowed = causal[None] & (docid[:, :, None] == docid[:, None, :])
    by_head = jnp.transpose(block_log, (0, 2, 1))
    gaps = by_head[:, :, :, None] - by_head[:, :, None, :]
    weight = jnp.where(allowed[:, None], jnp.exp(jnp.minimum(gaps, 0.0)), 0.0)
    scores = jnp.einsum(
        "nthd,nshd->nhts", query_blocks, key_blocks, preferred_element_type=jnp.float32
    )
    weights = (scores * weight).astype(jnp.bfloat16)
    intra = jnp.einsum("nhts,nshd->nthd", weights, value_blocks, preferred_element_type=jnp.float32)
    query_decayed = (
        query_blocks.astype(jnp.float32) * (jnp.exp(block_log) * reach_block[:, :, None])[..., None]
    ).astype(jnp.bfloat16)
    inter = jnp.einsum(
        "nthd,nhde->nthe",
        query_decayed,
        states.astype(jnp.bfloat16),
        preferred_element_type=jnp.float32,
    )
    return intra + inter


def carry_in(decay_all, s_end, devices):
    zero_state = jnp.zeros(s_end.shape, jnp.float32)

    def forward(index, pair):
        arrived = from_behind(pair[1], "ctx", 1)
        return (arrived, decay_all[:, None, None] * arrived + s_end)

    arrival, leaving = lax.fori_loop(0, devices - 1, forward, (zero_state, s_end))
    return arrival


def body(queries, key_rows, value_rows, log_decay, norm_gain, doc_lengths, packing):
    rows, width = queries.shape
    heads = log_decay.shape[1]
    head_size = width // heads
    blocks = rows // BLOCK
    devices = lax.axis_size("ctx")
    mine = lax.axis_index("ctx")
    total_blocks = packing.shape[0]
    capacity = (2 * blocks + devices - 1) // devices
    owners = (packing // blocks).reshape(devices, blocks)
    local = jnp.arange(blocks, dtype=jnp.int32)
    earlier_mask = local[:, None] < local[None, :]
    same_owner = owners[:, :, None] == owners[:, None, :]
    ranks = jnp.sum((same_owner & earlier_mask[None]).astype(jnp.int32), axis=1)
    my_owner = lax.dynamic_index_in_dim(owners, mine, 0, keepdims=False)
    my_rank = lax.dynamic_index_in_dim(ranks, mine, 0, keepdims=False)
    slot_of = my_owner * capacity + my_rank
    slot_ids = jnp.arange(devices * capacity, dtype=jnp.int32)
    matched = slot_of[None, :] == slot_ids[:, None]
    source = jnp.sum(matched.astype(jnp.int32) * local[None, :], axis=1)
    filled = jnp.any(matched, axis=1)

    def outgoing(values):
        columns = values.shape[1]
        picked = jnp.take(values.reshape(blocks, BLOCK, columns), source, axis=0)
        kept = jnp.where(filled[:, None, None], picked, jnp.zeros((), values.dtype))
        return kept.reshape(devices, capacity * BLOCK, columns)

    target = mine * blocks + local
    block_index = jnp.arange(total_blocks, dtype=jnp.int32)
    wanted = packing[None, :] == target[:, None]
    loader_block = jnp.sum(wanted.astype(jnp.int32) * block_index[None, :], axis=1)
    column = loader_block // blocks * capacity + jnp.take(ranks.reshape(-1), loader_block)

    def arriving(values):
        return jnp.take(values.reshape(devices * capacity, BLOCK, values.shape[2]), column, axis=0)

    starts = jnp.cumsum(doc_lengths) - doc_lengths
    positions = mine * rows + jnp.arange(rows, dtype=jnp.int32)
    first = (
        jnp.any(positions[:, None] == starts[None, :], axis=1)
        .astype(jnp.int32)
        .reshape(blocks, BLOCK)
    )
    docid = (
        jnp.sum((starts[None, :] <= positions[:, None]).astype(jnp.int32), axis=1) - 1
    ).reshape(blocks, BLOCK)
    got_queries, got_keys, got_values, received_decay = (
        lax.all_to_all(outgoing(queries), "ctx", split_axis=0, concat_axis=0, tiled=True),
        lax.all_to_all(outgoing(key_rows), "ctx", split_axis=0, concat_axis=0, tiled=True),
        lax.all_to_all(outgoing(value_rows), "ctx", split_axis=0, concat_axis=0, tiled=True),
        lax.all_to_all(outgoing(log_decay), "ctx", split_axis=0, concat_axis=0, tiled=True),
    )
    key_blocks = arriving(got_keys).reshape(blocks, BLOCK, heads, head_size)
    value_blocks = arriving(got_values).reshape(blocks, BLOCK, heads, head_size)
    decay_blocks = arriving(received_decay)
    block_log, reach_block, states, segment_log, reach_segment, decay_all, s_end = state_pass(
        key_blocks, value_blocks, decay_blocks, first, docid
    )
    arrival = carry_in(decay_all, s_end, devices)
    query_blocks = arriving(got_queries).reshape(blocks, BLOCK, heads, head_size)
    local_out = query_pass(
        query_blocks, key_blocks, value_blocks, block_log, reach_block, states, docid
    )
    scaled = (
        query_blocks.astype(jnp.float32)
        * (jnp.exp(segment_log) * reach_segment[:, :, None])[..., None]
    ).astype(jnp.bfloat16)
    carried = jnp.einsum(
        "nthd,hde->nthe", scaled, arrival.astype(jnp.bfloat16), preferred_element_type=jnp.float32
    )
    total = (local_out + carried).reshape(rows, width)
    squares = lax.psum(jnp.sum(total * total, axis=1), "head")
    columns_all = width * lax.axis_size("head")
    scale = lax.rsqrt(squares / columns_all + 1e-05)
    return (total * scale[:, None] * norm_gain[None, :]).astype(jnp.bfloat16)


def solution(mesh):
    placed = (
        P("ctx", "head"),
        P("ctx", "head"),
        P("ctx", "head"),
        P("ctx", "head"),
        P("head"),
        P(),
        P(),
    )
    one_head_each = mesh.shape["ctx"] == 8 and mesh.shape["head"] == 4
    return jax.shard_map(
        by_head if one_head_each else body, mesh=mesh, in_specs=placed, out_specs=P("ctx", "head"), check_vma=False
    )
```

```python
import functools

import jax
import jax.numpy as jnp
from jax import lax
from jax.experimental import pallas as pl
from jax.experimental.pallas import tpu as pltpu
from jax.sharding import PartitionSpec as P

BLOCK = 128
MESH = pl.DeviceIdType.MESH
ORDER = (4, 2, 5, 3, 6, 7, 1)
ARRAYS = 3
AHEAD = 2


def stage_list(blocks):
    stages = []
    slot = 0
    for low in range(0, blocks, 4):
        stages.append(((0, 1), low, 4, slot))
        slot += 2
    for low in range(0, blocks, 2):
        stages.append(((2,), low, 2, slot))
        slot += 1
    return stages


def flipped(me, bits):
    high, mid, low = me // 4, (me // 2) % 2, me % 2
    return (
        4 * ((high + bits // 4) % 2) + 2 * ((mid + bits // 2 % 2) % 2) + (low + bits % 2) % 2
    )


def turned(me, bits):
    swapped = 4 * (bits // 2 % 2) + 2 * (bits // 4) + bits % 2
    return bits + (swapped - bits) * (me % 2)


def contract(a, b, dim_a, dim_b):
    return lax.dot_general(
        a, b, (((dim_a,), (dim_b,)), ((), ())), preferred_element_type=jnp.float32
    )


def attention_kernel(
    peers,
    q_hbm,
    k_hbm,
    v_hbm,
    log_ref,
    length_ref,
    packing_ref,
    source_ref,
    out_hbm,
    total_ref,
    q_all,
    k_all,
    v_all,
    log_all,
    meta,
    q_decayed,
    intra,
    own,
    gate,
    states,
    out_all,
    squares,
    squares_in,
    share_in,
    send_sem,
    recv_sem,
    kept_sem,
    log_send,
    log_recv,
    out_send,
    out_recv,
    sq_send,
    sq_recv,
    share_send,
    share_recv,
):
    ctx, head = peers
    me = lax.axis_index("ctx")
    plane = lax.axis_index("head")
    blocks = log_ref.shape[1]
    total_blocks = ctx * blocks
    others = ORDER

    barrier = pltpu.get_barrier_semaphore()
    for bits in others:
        pl.semaphore_signal(
            barrier, inc=1, device_id=(flipped(me, bits), plane), device_id_type=MESH
        )
    for step in range(1, head):
        pl.semaphore_signal(
            barrier, inc=1, device_id=(me, (plane + step) % head), device_id_type=MESH
        )
    pl.semaphore_wait(barrier, ctx - 1 + head - 1)

    pairs = ((k_hbm, k_all), (v_hbm, v_all), (q_hbm, q_all))
    stages = stage_list(blocks)

    def columns(index):
        return pl.ds(pl.multiple_of(index * BLOCK, BLOCK), BLOCK)

    def span(index, low=0, count=blocks):
        return pl.ds(index * blocks + low, count)

    def remote(source, target, send, recv, there):
        return pltpu.make_async_remote_copy(
            src_ref=source,
            dst_ref=target,
            send_sem=send,
            recv_sem=recv,
            device_id=(there, plane),
            device_id_type=MESH,
        )

    def row_copies(stage, bits, arriving):
        arrays, low, count, slot = stages[stage]
        there = flipped(me, bits)
        origin = there if arriving else me
        return [
            remote(
                pairs[which][0].at[pl.ds(low, count), :, columns(there)],
                pairs[which][1].at[span(origin, low, count)],
                send_sem.at[slot + extra, bits],
                recv_sem.at[slot + extra, bits],
                there,
            )
            for extra, which in enumerate(arrays)
        ]

    def log_copy(bits, arriving):
        there = flipped(me, bits)
        origin = there if arriving else me
        return remote(
            log_ref.at[there], log_all.at[origin], log_send.at[bits], log_recv.at[bits], there
        )

    sequence = [turned(me, bits) for bits in others]

    def begin(stage):
        for bits in sequence:
            for copy in row_copies(stage, bits, False):
                copy.start()

    def sent(stage):
        for bits in others:
            for copy in row_copies(stage, bits, False):
                copy.wait_send()

    def arrived(stage):
        for bits in others:
            for copy in row_copies(stage, bits, True):
                copy.wait_recv()

    for bits in others:
        log_copy(bits, False).start()
    for stage in range(AHEAD):
        begin(stage)
    kept = [
        pltpu.make_async_copy(
            source.at[:, :, columns(me)], landing.at[span(me)], kept_sem.at[index]
        )
        for index, (source, landing) in enumerate(pairs)
    ]
    kept.append(pltpu.make_async_copy(log_ref.at[me], log_all.at[me], kept_sem.at[ARRAYS]))
    for copy in kept:
        copy.start()

    sub = lax.broadcasted_iota(jnp.int32, (BLOCK, BLOCK), 0)
    lane = lax.broadcasted_iota(jnp.int32, (BLOCK, BLOCK), 1)
    along = lax.broadcasted_iota(jnp.int32, (1, BLOCK), 1)

    starts = [jnp.int32(0)]
    for index in range(length_ref.shape[0] - 1):
        starts.append(starts[-1] + length_ref[index])

    def mark(block, carry):
        base = packing_ref[block] * BLOCK
        begins = jnp.full((1, BLOCK), -(1 << 24), jnp.int32)
        broken_at = jnp.full((1, BLOCK), BLOCK, jnp.int32)
        for start in starts:
            relative = jnp.broadcast_to(start - base, (1, BLOCK))
            begins = jnp.maximum(begins, jnp.where(relative <= along, relative, -(1 << 24)))
            broken_at = jnp.minimum(broken_at, jnp.where(relative >= 0, relative, BLOCK))
        meta[block, 0:1, :] = begins
        meta[block, 1:2, :] = broken_at
        meta[block, 2:3, :] = jnp.broadcast_to(begins[:, BLOCK - 1 :], (1, BLOCK))
        return carry

    lax.fori_loop(0, total_blocks, mark, 0)
    for copy in kept:
        copy.wait()
    for bits in others:
        log_copy(bits, True).wait_recv()

    def down(row):
        return jnp.transpose(jnp.broadcast_to(row, (BLOCK, BLOCK)))

    def key_blocks(places):
        rows = [log_all[there, index : index + 1, :] for there, index in places]
        ids = [there * blocks + index for there, index in places]
        marks = [meta[block, 2:3, :] for block in ids]
        keys = [k_all[block] for block in ids]
        values = [v_all[block] for block in ids]
        totals = [jnp.broadcast_to(row[:, BLOCK - 1 :], (1, BLOCK)) for row in rows]
        keeps = [
            down(jnp.where(along >= begin_at, jnp.exp(total - row), 0.0))
            for row, total, begin_at in zip(rows, totals, marks)
        ]
        decayed = [
            (key.astype(jnp.float32) * keep).astype(jnp.bfloat16)
            for key, keep in zip(keys, keeps)
        ]
        results = [contract(key, value, 0, 0) for key, value in zip(decayed, values)]
        for block, result, total, begin_at in zip(ids, results, totals, marks):
            own[block] = result
            gate[block] = jnp.where(begin_at < 0, jnp.exp(total), 0.0)

    def query_blocks(places):
        rows = [log_all[there, index : index + 1, :] for there, index in places]
        ids = [there * blocks + index for there, index in places]
        begins = [meta[block, 0:1, :] for block in ids]
        broken = [meta[block, 1:2, :] for block in ids]
        queries = [q_all[block] for block in ids]
        keys = [k_all[block] for block in ids]
        values = [v_all[block] for block in ids]
        scores = [contract(key, query, 1, 1) for key, query in zip(keys, queries)]
        downs = [down(row) for row in rows]
        reaches = [
            down(jnp.where(along < stop, jnp.exp(row), 0.0)) for row, stop in zip(rows, broken)
        ]
        weights = []
        for row, column, begin_at, score in zip(rows, downs, begins, scores):
            allowed = (sub >= begin_at) & (sub <= lane)
            factor = jnp.exp(jnp.minimum(row - column, 0.0))
            weights.append(jnp.where(allowed, score * factor, 0.0).astype(jnp.bfloat16))
        results = [contract(weight, value, 0, 0) for weight, value in zip(weights, values)]
        decayed = [
            (query.astype(jnp.float32) * reach).astype(jnp.bfloat16)
            for query, reach in zip(queries, reaches)
        ]
        for block, result, query in zip(ids, results, decayed):
            intra[block] = result
            q_decayed[block] = query

    def work(stage):
        arrays, low, count, slot = stages[stage]
        each = key_blocks if len(arrays) > 1 else query_blocks
        at_once = max(1, 4 // count)

        def several(step, carry):
            each(
                [
                    (step * at_once + extra, index)
                    for extra in range(at_once)
                    for index in range(low, low + count)
                ]
            )
            return carry

        lax.fori_loop(0, ctx // at_once, several, 0)

    def advance(step, state):
        for extra in range(4):
            place = step * 4 + extra
            block = source_ref[place]
            states[place] = state.astype(jnp.bfloat16)
            state = gate[block] * state + own[block]
        return state

    for stage in range(len(stages)):
        arrived(stage)
        if stage + AHEAD < len(stages):
            sent(stage)
            begin(stage + AHEAD)
        work(stage)
        if stage + 1 < len(stages) and len(stages[stage][0]) > len(stages[stage + 1][0]):
            zero_state = jnp.zeros((BLOCK, BLOCK), jnp.float32)
            lax.fori_loop(0, total_blocks // 4, advance, zero_state)

    ones = jnp.ones((8, BLOCK), jnp.bfloat16)

    def out_copy(bits, arriving):
        there = flipped(me, bits)
        origin = there if arriving else me
        return remote(
            out_all.at[span(there)],
            out_hbm.at[:, :, columns(origin)],
            out_send.at[bits],
            out_recv.at[bits],
            there,
        )

    def sq_copy(bits, arriving):
        there = flipped(me, bits)
        origin = there if arriving else me
        return remote(
            squares.at[there], squares_in.at[origin], sq_send.at[bits], sq_recv.at[bits], there
        )

    def finish(there):
        def several(step, carry):
            indices = [step * 4 + extra for extra in range(4)]
            places = [there * blocks + index for index in indices]
            ids = [source_ref[place] for place in places]
            terms = [intra[block] for block in ids]
            products = [
                contract(q_decayed[block], states[place], 1, 0) for block, place in zip(ids, places)
            ]
            results = [term + product for term, product in zip(terms, products)]
            summed = [
                contract(ones, (result * result).astype(jnp.bfloat16), 1, 1) for result in results
            ]
            for index, place, result, line in zip(indices, places, results, summed):
                out_all[place] = result.astype(jnp.bfloat16)
                squares[there, pl.ds(index, 1), :] = line[0:1]
            return carry

        lax.fori_loop(0, blocks // 4, several, 0)

    for index, bits in enumerate(sequence):
        finish(flipped(me, bits))
        if index < 4:
            out_copy(bits, False).start()
    for bits in others:
        sq_copy(bits, False).start()
    for bits in sequence[4:]:
        out_copy(bits, False).start()
    finish(me)
    kept_out = pltpu.make_async_copy(
        out_all.at[span(me)], out_hbm.at[:, :, columns(me)], kept_sem.at[0]
    )
    kept_out.start()
    summed = squares[me]
    for bits in others:
        sq_copy(bits, True).wait_recv()
        summed = summed + squares_in[flipped(me, bits)]
    share_in[plane] = summed

    def share_copy(step, slot):
        return pltpu.make_async_remote_copy(
            src_ref=share_in.at[plane],
            dst_ref=share_in.at[slot],
            send_sem=share_send.at[step],
            recv_sem=share_recv.at[step],
            device_id=(me, (plane + step) % head),
            device_id_type=MESH,
        )

    for step in range(1, head):
        share_copy(step, plane).start()
    total = summed
    for step in range(1, head):
        origin = (plane + head - step) % head
        share_copy(step, origin).wait_recv()
        total = total + share_in[origin]
    total_ref[...] = total
    for stage in range(len(stages) - AHEAD, len(stages)):
        sent(stage)
    kept_out.wait()
    for bits in others:
        out_copy(bits, True).wait_recv()
    for bits in others:
        log_copy(bits, False).wait_send()
        out_copy(bits, False).wait_send()
        sq_copy(bits, False).wait_send()
    for step in range(1, head):
        share_copy(step, plane).wait_send()


def by_head(queries, key_rows, value_rows, log_decay, norm_gain, doc_lengths, packing):
    rows, width = queries.shape
    heads = log_decay.shape[1]
    blocks = rows // BLOCK
    ctx = lax.axis_size("ctx")
    head = lax.axis_size("head")
    total_blocks = packing.shape[0]

    order = jnp.arange(BLOCK)
    lower = (order[:, None] >= order[None, :]).astype(jnp.bfloat16)
    logs = jnp.einsum(
        "ts,nsh->hnt",
        lower,
        log_decay.reshape(blocks, BLOCK, heads),
        preferred_element_type=jnp.float32,
    )
    places = jnp.arange(total_blocks, dtype=jnp.int32)
    source = jnp.sum(
        jnp.where(packing[None, :] == places[:, None], places[None, :], 0), axis=1
    ).astype(jnp.int32)

    def in_blocks(values):
        return values.reshape(blocks, BLOCK, width)

    copies = sum(len(stage[0]) for stage in stage_list(blocks))
    any_spec = pl.BlockSpec(memory_space=pl.ANY)
    vmem = pl.BlockSpec(memory_space=pltpu.VMEM)
    dma = pltpu.SemaphoreType.DMA
    out, squares = pl.pallas_call(
        functools.partial(attention_kernel, (ctx, head)),
        out_shape=(
            jax.ShapeDtypeStruct((blocks, BLOCK, width), jnp.bfloat16),
            jax.ShapeDtypeStruct((blocks, BLOCK), jnp.float32),
        ),
        in_specs=[any_spec] * 3 + [vmem] + [pl.BlockSpec(memory_space=pltpu.SMEM)] * 3,
        out_specs=(any_spec, vmem),
        scratch_shapes=[
            pltpu.VMEM((total_blocks, BLOCK, BLOCK), jnp.bfloat16),
            pltpu.VMEM((total_blocks, BLOCK, BLOCK), jnp.bfloat16),
            pltpu.VMEM((total_blocks, BLOCK, BLOCK), jnp.bfloat16),
            pltpu.VMEM((ctx, blocks, BLOCK), jnp.float32),
            pltpu.VMEM((total_blocks, 8, BLOCK), jnp.int32),
            pltpu.VMEM((total_blocks, BLOCK, BLOCK), jnp.bfloat16),
            pltpu.VMEM((total_blocks, BLOCK, BLOCK), jnp.float32),
            pltpu.VMEM((total_blocks, BLOCK, BLOCK), jnp.float32),
            pltpu.VMEM((total_blocks, 1, BLOCK), jnp.float32),
            pltpu.VMEM((total_blocks, BLOCK, BLOCK), jnp.bfloat16),
            pltpu.VMEM((total_blocks, BLOCK, BLOCK), jnp.bfloat16),
            pltpu.VMEM((ctx, blocks, BLOCK), jnp.float32),
            pltpu.VMEM((ctx, blocks, BLOCK), jnp.float32),
            pltpu.VMEM((head, blocks, BLOCK), jnp.float32),
            dma((copies, ctx)),
            dma((copies, ctx)),
            dma((ARRAYS + 1,)),
            dma((ctx,)),
            dma((ctx,)),
            dma((ctx,)),
            dma((ctx,)),
            dma((ctx,)),
            dma((ctx,)),
            dma((head,)),
            dma((head,)),
        ],
        compiler_params=pltpu.CompilerParams(
            collective_id=0, has_side_effects=True, vmem_limit_bytes=52 * 1024 * 1024
        ),
        name="attention_by_head",
    )(in_blocks(queries), in_blocks(key_rows), in_blocks(value_rows), logs, doc_lengths, packing, source)
    scale = lax.rsqrt(squares / (width * head) + 1e-05)
    normed = out.astype(jnp.float32) * scale[:, :, None] * norm_gain[None, None, :]
    return normed.astype(jnp.bfloat16).reshape(rows, width)


def from_behind(x, axis, by):
    count = lax.axis_size(axis)
    pairs = [(i, i + by) for i in range(count) if 0 <= i + by < count]
    return lax.ppermute(x, axis, pairs)


def state_pass(key_blocks, value_blocks, decay_blocks, first, docid):
    block_log = jnp.cumsum(decay_blocks.astype(jnp.float32), axis=1)
    block_total = block_log[:, -1, :]
    seen = jnp.cumsum(first, axis=1)
    reach_block = (seen == 0).astype(jnp.float32)
    unbroken = (seen[:, -1] == 0).astype(jnp.float32)
    same_last = (docid == docid[:, -1:]).astype(jnp.float32)
    keep = jnp.exp(block_total[:, None, :] - block_log) * same_last[:, :, None]
    key_decayed = (key_blocks.astype(jnp.float32) * keep[..., None]).astype(jnp.bfloat16)
    own = jnp.einsum(
        "nshd,nshe->nhde", key_decayed, value_blocks, preferred_element_type=jnp.float32
    )
    gate = jnp.exp(block_total) * unbroken[:, None]

    def advance(state, item):
        factor, term = item
        return (factor[:, None, None] * state + term, state)

    start = jnp.zeros(own.shape[1:], jnp.float32)
    s_end, states = lax.scan(advance, start, (gate, own))
    prior = jnp.cumsum(block_total, axis=0) - block_total
    segment_log = block_log + prior[:, None, :]
    block_starts = seen[:, -1]
    before = jnp.cumsum(block_starts) - block_starts
    reach_segment = (seen + before[:, None] == 0).astype(jnp.float32)
    clean = (jnp.sum(first) == 0).astype(jnp.float32)
    decay_all = jnp.exp(segment_log[-1, -1]) * clean
    return (block_log, reach_block, states, segment_log, reach_segment, decay_all, s_end)


def query_pass(query_blocks, key_blocks, value_blocks, block_log, reach_block, states, docid):
    length = docid.shape[1]
    order = jnp.arange(length)
    causal = order[:, None] >= order[None, :]
    allowed = causal[None] & (docid[:, :, None] == docid[:, None, :])
    by_head = jnp.transpose(block_log, (0, 2, 1))
    gaps = by_head[:, :, :, None] - by_head[:, :, None, :]
    weight = jnp.where(allowed[:, None], jnp.exp(jnp.minimum(gaps, 0.0)), 0.0)
    scores = jnp.einsum(
        "nthd,nshd->nhts", query_blocks, key_blocks, preferred_element_type=jnp.float32
    )
    weights = (scores * weight).astype(jnp.bfloat16)
    intra = jnp.einsum("nhts,nshd->nthd", weights, value_blocks, preferred_element_type=jnp.float32)
    query_decayed = (
        query_blocks.astype(jnp.float32) * (jnp.exp(block_log) * reach_block[:, :, None])[..., None]
    ).astype(jnp.bfloat16)
    inter = jnp.einsum(
        "nthd,nhde->nthe",
        query_decayed,
        states.astype(jnp.bfloat16),
        preferred_element_type=jnp.float32,
    )
    return intra + inter


def carry_in(decay_all, s_end, devices):
    zero_state = jnp.zeros(s_end.shape, jnp.float32)

    def forward(index, pair):
        arrived = from_behind(pair[1], "ctx", 1)
        return (arrived, decay_all[:, None, None] * arrived + s_end)

    arrival, leaving = lax.fori_loop(0, devices - 1, forward, (zero_state, s_end))
    return arrival


def body(queries, key_rows, value_rows, log_decay, norm_gain, doc_lengths, packing):
    rows, width = queries.shape
    heads = log_decay.shape[1]
    head_size = width // heads
    blocks = rows // BLOCK
    devices = lax.axis_size("ctx")
    mine = lax.axis_index("ctx")
    total_blocks = packing.shape[0]
    capacity = (2 * blocks + devices - 1) // devices
    owners = (packing // blocks).reshape(devices, blocks)
    local = jnp.arange(blocks, dtype=jnp.int32)
    earlier_mask = local[:, None] < local[None, :]
    same_owner = owners[:, :, None] == owners[:, None, :]
    ranks = jnp.sum((same_owner & earlier_mask[None]).astype(jnp.int32), axis=1)
    my_owner = lax.dynamic_index_in_dim(owners, mine, 0, keepdims=False)
    my_rank = lax.dynamic_index_in_dim(ranks, mine, 0, keepdims=False)
    slot_of = my_owner * capacity + my_rank
    slot_ids = jnp.arange(devices * capacity, dtype=jnp.int32)
    matched = slot_of[None, :] == slot_ids[:, None]
    source = jnp.sum(matched.astype(jnp.int32) * local[None, :], axis=1)
    filled = jnp.any(matched, axis=1)

    def outgoing(values):
        columns = values.shape[1]
        picked = jnp.take(values.reshape(blocks, BLOCK, columns), source, axis=0)
        kept = jnp.where(filled[:, None, None], picked, jnp.zeros((), values.dtype))
        return kept.reshape(devices, capacity * BLOCK, columns)

    target = mine * blocks + local
    block_index = jnp.arange(total_blocks, dtype=jnp.int32)
    wanted = packing[None, :] == target[:, None]
    loader_block = jnp.sum(wanted.astype(jnp.int32) * block_index[None, :], axis=1)
    column = loader_block // blocks * capacity + jnp.take(ranks.reshape(-1), loader_block)

    def arriving(values):
        return jnp.take(values.reshape(devices * capacity, BLOCK, values.shape[2]), column, axis=0)

    starts = jnp.cumsum(doc_lengths) - doc_lengths
    positions = mine * rows + jnp.arange(rows, dtype=jnp.int32)
    first = (
        jnp.any(positions[:, None] == starts[None, :], axis=1)
        .astype(jnp.int32)
        .reshape(blocks, BLOCK)
    )
    docid = (
        jnp.sum((starts[None, :] <= positions[:, None]).astype(jnp.int32), axis=1) - 1
    ).reshape(blocks, BLOCK)
    got_queries, got_keys, got_values, received_decay = (
        lax.all_to_all(outgoing(queries), "ctx", split_axis=0, concat_axis=0, tiled=True),
        lax.all_to_all(outgoing(key_rows), "ctx", split_axis=0, concat_axis=0, tiled=True),
        lax.all_to_all(outgoing(value_rows), "ctx", split_axis=0, concat_axis=0, tiled=True),
        lax.all_to_all(outgoing(log_decay), "ctx", split_axis=0, concat_axis=0, tiled=True),
    )
    key_blocks = arriving(got_keys).reshape(blocks, BLOCK, heads, head_size)
    value_blocks = arriving(got_values).reshape(blocks, BLOCK, heads, head_size)
    decay_blocks = arriving(received_decay)
    block_log, reach_block, states, segment_log, reach_segment, decay_all, s_end = state_pass(
        key_blocks, value_blocks, decay_blocks, first, docid
    )
    arrival = carry_in(decay_all, s_end, devices)
    query_blocks = arriving(got_queries).reshape(blocks, BLOCK, heads, head_size)
    local_out = query_pass(
        query_blocks, key_blocks, value_blocks, block_log, reach_block, states, docid
    )
    scaled = (
        query_blocks.astype(jnp.float32)
        * (jnp.exp(segment_log) * reach_segment[:, :, None])[..., None]
    ).astype(jnp.bfloat16)
    carried = jnp.einsum(
        "nthd,hde->nthe", scaled, arrival.astype(jnp.bfloat16), preferred_element_type=jnp.float32
    )
    total = (local_out + carried).reshape(rows, width)
    squares = lax.psum(jnp.sum(total * total, axis=1), "head")
    columns_all = width * lax.axis_size("head")
    scale = lax.rsqrt(squares / columns_all + 1e-05)
    return (total * scale[:, None] * norm_gain[None, :]).astype(jnp.bfloat16)


def solution(mesh):
    placed = (
        P("ctx", "head"),
        P("ctx", "head"),
        P("ctx", "head"),
        P("ctx", "head"),
        P("head"),
        P(),
        P(),
    )
    one_head_each = mesh.shape["ctx"] == 8 and mesh.shape["head"] == 4
    return jax.shard_map(
        by_head if one_head_each else body, mesh=mesh, in_specs=placed, out_specs=P("ctx", "head"), check_vma=False
    )
```
